32 devices in a mesh: gx: 8 (over z, x), gy: 4 (over y, core).
Axes of the slice: x: 2, y: 2, z: 4, core: 2. Of those that a mesh axis runs over, the one named last changes fastest.
Arguments:
- theta: float32 [80, 512, 512], P(None, 'gx', 'gy'), may hold values from -6 to 6
- wind_u: float32 [80, 512, 512], P(None, 'gx', 'gy'), may hold values from -1 to 1
- wind_v: float32 [80, 512, 512], P(None, 'gx', 'gy'), may hold values from -1 to 1
- level_set: float32 [8, 4, 16, 128, 128], P('gx', 'gy'), may hold values from -6 to 6
- fuel_load: float32 [8, 4, 16, 128, 128], P('gx', 'gy'), may hold values from 0.5 to 1.5
- spread_base: float32 [8, 4, 16, 128, 128], P('gx', 'gy'), may hold values from 0.3 to 3
- tile_owner: int32 [8, 4, 16], P('gx', 'gy'), may hold values from 0 to 7, as said below
- tile_place: int32 [8, 4, 16], P('gx', 'gy'), may hold values from 0 to 511, as said below
Outputs:
- theta_next: float32 [80, 512, 512], P(None, 'gx', 'gy')
- level_next: float32 [8, 4, 16, 128, 128], P('gx', 'gy')
- fuel_next: float32 [8, 4, 16, 128, 128], P('gx', 'gy')
The draws below stay inside these ranges and needn't reach their ends.
Inputs may be any that keep to these rules, and one draw needn't show every extreme that they name: Every tile of device (i, j) lies in the block of a device (tile_owner, j) of the same gy index; at most 2 tiles of one device lie in one owner's block, and in every draw some owner of each gy index holds exactly 2 tiles from every device of that index. `tile_place`: no two computed tiles have the same owner and place.
All inputs are finite; a program needn't handle non-finite values.
Results may differ from the reference program's by a relative error of at most 0.0003.
Values sent between devices are 32-bit elements; how exact they have to be, the bound alone decides.
A program may use at most 128 MiB of HBM per device.

```python
import math
import jax
import jax.numpy as jnp
from jax import lax

CX = 64
CY = 128
LZ = 80
TA = 4
R = 32
KSUB = 6
CAP = 2
TPD = 16
S = 128
FIRE_X = 8
FIRE_Y = 4
NXA = 512
NYA = 512


def tile_lists(key):
    cycle = NXA // CX
    rows = NYA // CY
    places_count = CX // TA * (CY // TA)
    owner_key = jax.random.fold_in(key, 101)
    hot_key = jax.random.fold_in(key, 102)
    place_key = jax.random.fold_in(key, 103)
    pool = jnp.repeat(jnp.arange(1, cycle, dtype=jnp.int32), CAP)
    owner_keys = jax.random.split(owner_key, cycle * rows)

    def pick(single):
        return jax.random.permutation(single, pool)[:TPD - CAP]
    others = jax.vmap(pick)(owner_keys).reshape(cycle, rows, TPD - CAP)
    first = jnp.zeros((cycle, rows, CAP), jnp.int32)
    shifted = jnp.concatenate([first, others], axis=2)
    hottest = jax.random.randint(hot_key, (rows,), 0, cycle)
    owners = ((shifted + hottest[None, :, None]) % cycle).astype(jnp.int32)
    same_owner = owners[:, :, :, None] == owners[:, :, None, :]
    earlier = jnp.arange(TPD)[None, :] < jnp.arange(TPD)[:, None]
    slot_rank = jnp.sum(jnp.logical_and(same_owner, earlier[None, None]), axis=3).astype(jnp.int32)
    place_keys = jax.random.split(place_key, cycle * rows)
    orders = jax.vmap(lambda single: jax.random.permutation(single, places_count))(place_keys).reshape(cycle, rows, places_count)
    source = jnp.arange(cycle, dtype=jnp.int32)[:, None, None]
    row_index = jnp.arange(rows, dtype=jnp.int32)[None, :, None]
    places = orders[owners, row_index, source * CAP + slot_rank].astype(jnp.int32)
    return (owners, places)


def draw_tile_owner(key, part):
    return tile_lists(key)[0]


def draw_tile_place(key, part):
    return tile_lists(key)[1]


def level_of(own_key, shape, cuts, low, top_value):
    def one(position, shards_of):
        heights = jax.random.uniform(jax.random.fold_in(jax.random.fold_in(own_key, 6), position), (shards_of,), jnp.float32, low / len(cuts), top_value / len(cuts))
        return jnp.repeat(jnp.exp(heights), shape[position] // shards_of).reshape((-1,) + (1,) * (len(shape) - position - 1))

    loudness = one(*cuts[0])
    for cut in cuts[1:]:
        loudness = loudness * one(*cut)
    return loudness


def centred(key, dims, deviation, most, cuts=(), kind=jnp.bfloat16):
    values = deviation * jax.random.normal(key, dims, jnp.float32)
    if cuts:
        values = values * level_of(key, dims, cuts, -0.22, 0.18)
    return jnp.clip(values, -most, most).astype(kind)


def setup_inputs(seed: int = 0) -> dict:
    key_of = jax.random.split(jax.random.key(seed), 9)
    theta = centred(key_of[0], (LZ, NXA, NYA), 1.0, 6.0, ((1, 8), (2, 4)), jnp.float32)
    wind_u = jnp.clip(jax.random.uniform(key_of[1], (LZ, NXA, NYA), jnp.float32, -1.0, 1.0) * level_of(key_of[1], (LZ, NXA, NYA), ((1, 8), (2, 4)), -0.4, 0.0), -1.0, 1.0)
    wind_v = jnp.clip(jax.random.uniform(key_of[2], (LZ, NXA, NYA), jnp.float32, -1.0, 1.0) * level_of(key_of[2], (LZ, NXA, NYA), ((1, 8), (2, 4)), -0.4, 0.0), -1.0, 1.0)
    level_set = centred(key_of[3], (FIRE_X, FIRE_Y, TPD, S, S), 1.0, 6.0, ((0, 8), (1, 4)), jnp.float32)
    fuel_load = jnp.clip(0.5 + 1.0 * jax.random.uniform(key_of[4], (FIRE_X, FIRE_Y, TPD, S, S), jnp.float32) ** level_of(key_of[4], (FIRE_X, FIRE_Y, TPD, S, S), ((0, 8), (1, 4)), -0.2, 0.2), 0.5, 1.5)
    spread_base = jnp.clip(jnp.exp(math.log(3.0) - 2.3025851 * jax.random.uniform(key_of[5], (FIRE_X, FIRE_Y, TPD, S, S), jnp.float32) ** level_of(key_of[5], (FIRE_X, FIRE_Y, TPD, S, S), ((0, 8), (1, 4)), -0.2, 0.2)), 0.3, 3.0)
    tile_owner = draw_tile_owner(jax.random.fold_in(key_of[8], 71), 0)
    tile_place = draw_tile_place(jax.random.fold_in(key_of[8], 71), 0)
    return {"theta": theta, "wind_u": wind_u, "wind_v": wind_v, "level_set": level_set, "fuel_load": fuel_load, "spread_base": spread_base, "tile_owner": tile_owner, "tile_place": tile_place}


time_step = 0.03
diffusion = 0.15
burn_rate = 0.15
sharpness = 2.0
regular = 0.01
courant = 0.4
heat_gain = 2.0

def interp_table():
    where_fine = (jnp.arange(S, dtype=jnp.float32) + 0.5) / R + 0.5
    columns = jnp.arange(TA + 2, dtype=jnp.float32)
    return jnp.maximum(0.0, 1.0 - jnp.abs(where_fine[:, None] - columns[None, :]))

def average_table():
    block_of = jnp.arange(S, dtype=jnp.int32) // R
    coarse = jnp.arange(TA, dtype=jnp.int32)
    return jnp.where(coarse[:, None] == block_of[None, :], 1.0 / R, 0.0).astype(jnp.float32)

def fire_tile(level, fuel, base, wind, average):
    heat = jnp.zeros_like(fuel)
    for substep in range(KSUB):
        padded = jnp.pad(level, 1, mode='edge')
        grad_x = 0.5 * (padded[2:, 1:-1] - padded[:-2, 1:-1])
        grad_y = 0.5 * (padded[1:-1, 2:] - padded[1:-1, :-2])
        laplace = padded[2:, 1:-1] + padded[:-2, 1:-1] + padded[1:-1, 2:] + padded[1:-1, :-2] - 4.0 * level
        length = jnp.sqrt(grad_x * grad_x + grad_y * grad_y + regular)
        along = (wind[0] * grad_x + wind[1] * grad_y) / length
        speed = base * jnp.maximum(1.0 + along, 0.0)
        level = level - time_step * speed * length + diffusion * laplace
        used = burn_rate * fuel * jax.nn.sigmoid(-sharpness * level)
        fuel = fuel - used
        heat = heat + used
    flux = jnp.dot(jnp.dot(average, heat, precision=lax.Precision.HIGHEST), average.T, precision=lax.Precision.HIGHEST)
    return (level, fuel, flux)

def reference(theta, wind_u, wind_v, level_set, fuel_load, spread_base, tile_owner, tile_place):
    cycle = NXA // CX
    rows = NYA // CY
    tiles_y = CY // TA
    interp = interp_table()
    average = average_table()
    surface = jnp.pad(jnp.stack([wind_u[0], wind_v[0]]), ((0, 0), (1, 1), (1, 1)))
    row_index = jnp.arange(rows, dtype=jnp.int32)[None, :, None]
    start_x = (tile_owner * CX + tile_place // tiles_y * TA).astype(jnp.int32)
    start_y = (row_index * CY + tile_place % tiles_y * TA).astype(jnp.int32)
    start_x = start_x.reshape(cycle * rows, TPD)
    start_y = start_y.reshape(cycle * rows, TPD)

    def one_device(items):
        level, fuel, base, first_x, first_y = items

        def cut(left, bottom):
            return lax.dynamic_slice(surface, (jnp.int32(0), left.astype(jnp.int32), bottom.astype(jnp.int32)), (2, TA + 2, TA + 2))
        patches = jax.vmap(cut)(first_x, first_y)
        winds = jnp.einsum('ak,tckl,bl->tcab', interp, patches, interp, precision=lax.Precision.HIGHEST)
        return jax.vmap(lambda a, b, c, d: fire_tile(a, b, c, d, average))(level, fuel, base, winds)
    shaped = (level_set.reshape(cycle * rows, TPD, S, S), fuel_load.reshape(cycle * rows, TPD, S, S), spread_base.reshape(cycle * rows, TPD, S, S), start_x, start_y)
    level_out, fuel_out, fluxes = lax.map(one_device, shaped)
    offsets = jnp.arange(TA, dtype=jnp.int32)
    index_x = start_x.reshape(-1)[:, None, None] + offsets[None, :, None]
    index_y = start_y.reshape(-1)[:, None, None] + offsets[None, None, :]
    index_x = jnp.broadcast_to(index_x, (cycle * rows * TPD, TA, TA))
    index_y = jnp.broadcast_to(index_y, (cycle * rows * TPD, TA, TA))
    field = jnp.zeros((NXA, NYA), jnp.float32).at[index_x, index_y].add(fluxes.reshape(-1, TA, TA))
    padded = jnp.pad(theta, ((0, 0), (1, 1), (1, 1)))
    centre = theta
    advect = courant * (jnp.maximum(wind_u, 0.0) * (centre - padded[:, :-2, 1:-1]) + jnp.minimum(wind_u, 0.0) * (padded[:, 2:, 1:-1] - centre) + jnp.maximum(wind_v, 0.0) * (centre - padded[:, 1:-1, :-2]) + jnp.minimum(wind_v, 0.0) * (padded[:, 1:-1, 2:] - centre))
    profile = jnp.exp(-(jnp.arange(LZ, dtype=jnp.float32) + 0.5) / (LZ / 4.0))
    theta_next = theta - advect + heat_gain * field[None, :, :] * profile[:, None, None]
    shape_out = (cycle, rows, TPD, S, S)
    return (theta_next, level_out.reshape(shape_out), fuel_out.reshape(shape_out))
```

```python
import functools

import jax
import jax.numpy as jnp
from jax import lax
from jax.experimental import pallas as pl
from jax.experimental.pallas import tpu as pltpu
from jax.sharding import PartitionSpec as P

TA = 4
R = 32
KSUB = 6
CAP = 2
TPD = 16
S = 128
BX = 64
BY = 128
GROUP = 8

MESH = pl.DeviceIdType.MESH
F32 = jnp.float32
BF16 = jnp.bfloat16


def iota(shape, dim):
    return lax.broadcasted_iota(jnp.int32, shape, dim)


def pieces(x):
    high = x.astype(BF16)
    rest = x - high.astype(F32)
    middle = rest.astype(BF16)
    low = (rest - middle.astype(F32)).astype(BF16)
    return (high, middle, low)


def dot(a, b):
    return jnp.dot(a, b, preferred_element_type=F32)


def dot_left_exact(a, b):
    a = a.astype(BF16)
    high, middle, low = pieces(b)
    return dot(a, high) + (dot(a, middle) + dot(a, low))


def dot_right_exact(a, b):
    b = b.astype(BF16)
    high, middle, low = pieces(a)
    return dot(high, b) + (dot(middle, b) + dot(low, b))


def interp_weight(fine, column):
    where_fine = (fine.astype(F32) + 0.5) / R + 0.5
    return jnp.maximum(0.0, 1.0 - jnp.abs(where_fine - column.astype(F32)))


def kernel(
    G, H, LZ,
    theta_hbm, u_hbm, v_hbm, level_hbm, fuel_hbm, base_hbm, owner_ref, place_ref,
    part_hbm, level_out, fuel_out, field_ref,
    th, uu, vv, part, lev, spare, fin, fout, base, wind, wide, small, rows, code_col,
    req_out, req_in, rep_out, rep_in, flux_out, flux_in,
    yw_out, yw_in, yth_out, yth_in, xth_out, xth_in,
    in_sem, lev_sem, fuel_sem, part_sem,
    req_send, req_recv, rep_send, rep_recv, flux_send, flux_recv,
    yw_send, yw_recv, th_send, th_recv,
):
    Q = G * CAP
    i = lax.axis_index("gx")
    j = lax.axis_index("gy")

    def gx(offset):
        return lax.rem(i + (offset % G), G)

    def gy(offset):
        return lax.rem(j + (offset % H), H)

    loads = [
        pltpu.make_async_copy(u_hbm.at[0], uu.at[0], in_sem.at[0]),
        pltpu.make_async_copy(v_hbm.at[0], vv.at[0], in_sem.at[1]),
        pltpu.make_async_copy(theta_hbm, th.at[:, 8:8 + BX, :], in_sem.at[2]),
        pltpu.make_async_copy(u_hbm.at[1:], uu.at[1:], in_sem.at[3]),
        pltpu.make_async_copy(v_hbm.at[1:], vv.at[1:], in_sem.at[4]),
        pltpu.make_async_copy(level_hbm.at[0, 0], lev.at[:, 8:8 + S, :], in_sem.at[5]),
        pltpu.make_async_copy(fuel_hbm.at[0, 0], fin, in_sem.at[6]),
        pltpu.make_async_copy(base_hbm.at[0, 0], base, in_sem.at[7]),
    ]
    for load in loads:
        load.start()

    corners = [(0, 1), (0, -1), (-1, 1), (-1, -1), (1, 1), (1, -1)]
    barrier = pltpu.get_barrier_semaphore()
    for o in range(1, G):
        pl.semaphore_signal(barrier, inc=1, device_id=(gx(o), j), device_id_type=MESH)
    for dx, dy in corners:
        pl.semaphore_signal(barrier, inc=1, device_id=(gx(dx), gy(dy)), device_id_type=MESH)

    lane = iota((8, 128), 1)
    lane16 = lane & (TPD - 1)
    sub16 = iota((TPD, 128), 0)
    own_row = jnp.zeros((8, 128), jnp.int32)
    place_row = jnp.zeros((8, 128), jnp.int32)
    own_col = jnp.zeros((TPD, 128), jnp.int32)
    for t in range(TPD):
        own_row = jnp.where(lane16 == t, owner_ref[0, 0, t], own_row)
        place_row = jnp.where(lane16 == t, place_ref[0, 0, t], place_row)
        own_col = jnp.where(sub16 == t, owner_ref[0, 0, t], own_col)
    rank_row = jnp.zeros((8, 128), jnp.int32)
    rank_col = jnp.zeros((TPD, 128), jnp.int32)
    for t in range(TPD):
        rank_row += jnp.where(
            jnp.logical_and(own_row == owner_ref[0, 0, t], lane16 > t), 1, 0)
        rank_col += jnp.where(
            jnp.logical_and(own_col == owner_ref[0, 0, t], sub16 > t), 1, 0)

    def code_of(owner, rank):
        away = owner - i
        return jnp.where(away < 0, away + G, away) * CAP + rank

    code_row = code_of(own_row, rank_row)
    code_col[...] = code_of(own_col, rank_col)

    row1 = code_row[0:1]
    place1 = place_row[0:1]
    wanted = jnp.where(
        jnp.logical_and(row1 == iota((Q, 128), 0), iota((Q, 128), 1) < TPD),
        place1 + 1, 0).astype(F32)
    asked = jnp.broadcast_to(jnp.sum(wanted, axis=1, keepdims=True) - 1.0, (Q, 128))

    loads[0].wait()
    loads[1].wait()
    for o in range(G):
        req_out[o, 0:2, :] = asked[2 * o:2 * o + 2]
        edge = 0 if o == G - 1 else BX - 1
        req_out[o, 2:3, :] = uu[0, edge:edge + 1, :]
        req_out[o, 3:4, :] = vv[0, edge:edge + 1, :]
    packed = jnp.zeros((8, 128), F32)
    for g in range(16):
        source = uu if g < 8 else vv
        cell = source[0, 8 * (g % 8):8 * (g % 8) + 8, :]
        packed = jnp.where((lane >> 1) == g, pltpu.roll(cell, 2 * g + 1, 1), packed)
    yw_out[...] = packed

    pl.semaphore_wait(barrier, G - 1 + len(corners))

    def to_peer(o, out, into, send, recv):
        return pltpu.make_async_remote_copy(
            src_ref=out, dst_ref=into, send_sem=send, recv_sem=recv,
            device_id=(gx(o), j), device_id_type=MESH)

    requests = [
        to_peer(o, req_out.at[o], req_in.at[o], req_send.at[o], req_recv.at[o])
        for o in range(1, G)
    ]
    winds = [
        pltpu.make_async_remote_copy(
            src_ref=yw_out, dst_ref=yw_in.at[n], send_sem=yw_send.at[n],
            recv_sem=yw_recv.at[n], device_id=(gx(dx), gy(dy)), device_id_type=MESH)
        for n, (dx, dy) in enumerate(corners)
    ]
    for copy in requests + winds:
        copy.start()
    req_in[0] = req_out[0]

    fine_of = iota((2 * S, 48), 0)
    slot_of = iota((2 * S, 48), 1) & 15
    column = slot_of - 6 * (fine_of >> 7)
    a3 = jnp.where(
        jnp.logical_and(column >= 0, column < 6),
        interp_weight(fine_of & (S - 1), column), 0.0).astype(BF16)
    wide[...] = a3

    loads[2].wait()

    def pack(zz, carry):
        acc = jnp.zeros((8, 128), F32)
        for zl in range(GROUP):
            z = zz * GROUP + zl
            for g in range(8):
                n = zl * 8 + g
                cell = th[z, 8 + 8 * g:16 + 8 * g, :]
                acc = jnp.where((lane >> 1) == n, pltpu.roll(cell, (2 * n + 1) % 128, 1), acc)
            xth_out[0, pl.ds(z, 1), :] = th[z, 7 + BX:8 + BX, :]
            xth_out[1, pl.ds(z, 1), :] = th[z, 8:9, :]
        yth_out[pl.ds(pl.multiple_of(zz * 8, 8), 8), :] = acc
        return carry

    lax.fori_loop(0, LZ // GROUP, pack, 0)
    halos = []
    for n, (out, into, dx, dy) in enumerate([
        (xth_out.at[0], xth_in.at[0], 1, 0),
        (xth_out.at[1], xth_in.at[1], -1, 0),
        (yth_out, yth_in.at[0], 0, 1),
        (yth_out, yth_in.at[1], 0, -1),
    ]):
        halos.append(pltpu.make_async_remote_copy(
            src_ref=out, dst_ref=into, send_sem=th_send.at[n], recv_sem=th_recv.at[n],
            device_id=(gx(dx), gy(dy)), device_id_type=MESH))
    for copy in halos:
        copy.start()

    for copy in winds:
        copy.wait_recv()
    for copy in requests:
        copy.wait_recv()
    odd = (lane & 1) == 1
    ends = jnp.logical_or(lane == 0, lane == 127)
    is_first = i == 0
    is_last = i == G - 1
    south_ok = jnp.where(j > 0, 1.0, 0.0).astype(F32)
    north_ok = jnp.where(j < H - 1, 1.0, 0.0).astype(F32)
    west_ok = jnp.where(i > 0, 1.0, 0.0).astype(F32)
    east_ok = jnp.where(i < G - 1, 1.0, 0.0).astype(F32)

    def both(south, north):
        return jnp.where(odd, north * north_ok, south * south_ok)

    def unpack(mixed, n):
        return pltpu.roll(mixed, (127 - 2 * n) % 128, 1)

    sub = iota((8, 128), 0)
    here = both(yw_in[0], yw_in[1])
    east = both(yw_in[2], yw_in[3]) * east_ok
    west = both(yw_in[4], yw_in[5]) * west_ok
    surface = []
    for c, source in ((0, uu), (1, vv)):
        zeros = jnp.zeros((8, 128), F32)
        left = [source[0]]
        right = [jnp.where(ends, unpack(here, 8 * c + g), 0.0) for g in range(8)]
        east_row = req_in[G - 1, 2 + c:3 + c, :] * east_ok
        west_row = req_in[1, 2 + c:3 + c, :] * west_ok
        left.append(jnp.where(sub == 0, east_row, 0.0))
        left += [zeros] * 6
        left.append(jnp.where(sub == 7, west_row, 0.0))
        right.append(jnp.where(jnp.logical_and(ends, sub == 0), unpack(east, 8 * c), 0.0))
        right += [zeros] * 6
        right.append(jnp.where(jnp.logical_and(ends, sub == 7), unpack(west, 8 * c + 7), 0.0))
        surface.append(jnp.concatenate(
            [jnp.concatenate(left, axis=0), jnp.concatenate(right, axis=0)], axis=1))

    lane_q = iota((16, 128), 1)
    k_q = iota((16, 128), 0)
    pick = ([], [])
    masks = []
    later = []
    for q in range(Q):
        place = req_in[q // CAP, q % CAP:q % CAP + 1, :].astype(jnp.int32)
        x0 = (place >> 5) * TA
        y0 = (place & 31) * TA
        for c in range(2):
            m = k_q - 6 * c
            hit = jnp.logical_and(
                lane_q == ((x0 - 1 + m) & 127), jnp.logical_and(m >= 0, m < 6))
            pick[c].append(jnp.where(hit, 1.0, 0.0))
        low = (lane_q - (y0 - 1)) & 255
        high = (lane_q + 128 - (y0 - 1)) & 255
        masks.append(jnp.concatenate(
            [jnp.where(low < 6, 1.0, 0.0), jnp.where(high < 6, 1.0, 0.0)], axis=1))
        later.append(jnp.broadcast_to((y0 & 4) != 0, (16, 128)))
    found = (dot_left_exact(jnp.concatenate(pick[0], axis=0), surface[0])
             + dot_left_exact(jnp.concatenate(pick[1], axis=0), surface[1]))
    found = found * jnp.concatenate(masks, axis=0)
    c_e = iota((256, 256), 0)
    l_e = iota((256, 256), 1)
    shift = jnp.where(l_e < 128, 1, 5)
    squeeze = jnp.where(((c_e + shift) & 7) == (l_e & 7), 1.0, 0.0)
    tight = dot_right_exact(found, squeeze)
    own_lanes = (lane_q >> 3) == k_q
    for q in range(Q):
        block = tight[16 * q:16 * q + 16]
        chosen = jnp.where(later[q], block[:, 128:], block[:, :128])
        rep_out[q // CAP, q % CAP:q % CAP + 1, :] = jnp.sum(
            jnp.where(own_lanes, chosen, 0.0), axis=0, keepdims=True)
    replies = [
        to_peer(-o, rep_out.at[o], rep_in.at[o], rep_send.at[o], rep_recv.at[o])
        for o in range(1, G)
    ]
    for copy in replies:
        copy.start()
    rep_in[0] = rep_out[0]

    def advect(zz, carry):
        rows_of = pl.ds(pl.multiple_of(zz * 8, 8), 8)
        mixed = both(yth_in[0, rows_of, :], yth_in[1, rows_of, :])
        for zl in range(GROUP):
            z = zz * GROUP + zl
            th[z, 7:8, :] = xth_in[0, pl.ds(z, 1), :] * west_ok
            th[z, 8 + BX:9 + BX, :] = xth_in[1, pl.ds(z, 1), :] * east_ok
            for g in range(8):
                at = 8 + 8 * g
                centre = th[z, at:at + 8, :]
                before = th[z, at - 1:at + 7, :]
                after = th[z, at + 1:at + 9, :]
                edge = unpack(mixed, zl * 8 + g)
                south = pltpu.roll(jnp.where(lane == 127, edge, centre), 1, 1)
                north = pltpu.roll(jnp.where(lane == 0, edge, centre), 127, 1)
                u = uu[z, 8 * g:8 * g + 8, :]
                v = vv[z, 8 * g:8 * g + 8, :]
                total = (jnp.maximum(u, 0.0) * (centre - before)
                         + jnp.minimum(u, 0.0) * (after - centre)
                         + jnp.maximum(v, 0.0) * (centre - south)
                         + jnp.minimum(v, 0.0) * (north - centre))
                part[z, 8 * g:8 * g + 8, :] = centre - 0.4 * total
        store(zz).start()
        return carry

    def store(zz):
        levels = pl.ds(zz * GROUP, GROUP)
        return pltpu.make_async_copy(part.at[levels], part_hbm.at[levels], part_sem.at[zz])

    groups = LZ // GROUP
    first_groups = groups // 2
    for copy in halos:
        copy.wait_recv()
    loads[3].wait()
    loads[4].wait()
    lax.fori_loop(0, first_groups, advect, 0)

    for copy in replies:
        copy.wait_recv()
    answers = jnp.concatenate([rep_in[o] for o in range(G)], axis=0)
    is_slot = jnp.where(code_col[:, :Q] == iota((TPD, Q), 1), 1.0, 0.0)
    patch = dot_left_exact(is_slot, answers)
    spread = jnp.concatenate(
        [jnp.where(own_lanes, patch[t:t + 1], 0.0) for t in range(TPD)], axis=0)
    by_y = jnp.where(
        (iota((128, 128), 0) & 7) < 6,
        interp_weight(iota((128, 128), 1), iota((128, 128), 0) & 7), 0.0)
    along_y = dot_right_exact(spread, by_y)
    high, middle, low = pieces(along_y)
    for t in range(TPD):
        small[t, 0:16, :] = high[16 * t:16 * t + 16]
        small[t, 16:32, :] = middle[16 * t:16 * t + 16]
        small[t, 32:48, :] = low[16 * t:16 * t + 16]

    for load in loads[5:]:
        load.wait()
    pair = 2
    lane_c = iota((R, 128), 1)
    first_lane = lane_c == 0
    last_lane = lane_c == 127

    def level_store(t):
        return pltpu.make_async_copy(
            lev.at[t, 8:8 + S, :], level_out.at[0, 0, t], lev_sem.at[t])

    def fuel_store(t):
        return pltpu.make_async_copy(fout.at[t], fuel_out.at[0, 0, t], fuel_sem.at[t])

    def fire(step, carry):
        for p in range(pair):
            t = step * pair + p
            wind[p] = dot(wide[...], small[t])
            lev[t, 7:8, :] = lev[t, 8:9, :]
            lev[t, 8 + S:9 + S, :] = lev[t, 7 + S:8 + S, :]
        for k in range(KSUB):
            for p in range(pair):
                t = step * pair + p
                old = lev.at[t] if k % 2 == 0 else spare.at[p]
                new = spare.at[p] if k % 2 == 0 else lev.at[t]
                for b in range(S // R):
                    at = 8 + R * b
                    centre = old[at:at + R, :]
                    before = old[at - 1:at - 1 + R, :]
                    after = old[at + 1:at + 1 + R, :]
                    left = jnp.where(first_lane, centre, pltpu.roll(centre, 1, 1))
                    right = jnp.where(last_lane, centre, pltpu.roll(centre, 127, 1))
                    dx = after - before
                    dy = right - left
                    around = (after + before) + (right + left)
                    square = dx * dx + dy * dy + 0.04
                    length = square * lax.rsqrt(square)
                    blown = (wind[p, R * b:R * b + R, :] * dx
                             + wind[p, S + R * b:S + R * b + R, :] * dy)
                    rate = (0.015 * base[t, R * b:R * b + R, :]) * jnp.maximum(
                        length + blown, 0.0)
                    level = (0.4 * centre + 0.15 * around) - rate
                    new[at:at + R, :] = level
                    if k < KSUB - 1:
                        if b == 0:
                            new[7:8, :] = level[0:1]
                        if b == S // R - 1:
                            new[8 + S:9 + S, :] = level[R - 1:R]
                    before_fuel = (fin if k == 0 else fout)[t, R * b:R * b + R, :]
                    fuel = before_fuel * (0.925 + 0.075 * jnp.tanh(level))
                    fout[t, R * b:R * b + R, :] = fuel
                    if k == KSUB - 1:
                        burnt = fin[t, R * b:R * b + R, :] - fuel
                        rows[b, pl.ds(t, 1), :] = jnp.sum(burnt, axis=0, keepdims=True)
        for p in range(pair):
            t = step * pair + p
            level_store(t).start()
            fuel_store(t).start()
        return carry

    lax.fori_loop(0, TPD // pair, fire, 0)

    l_m = iota((128, 128), 0)
    c_m = iota((128, 128), 1)
    mean = jnp.where((l_m >> 5) == (c_m & 3), 1.0 / (R * R), 0.0)
    fluxes = dot_right_exact(jnp.concatenate([rows[b] for b in range(TA)], axis=0), mean)
    slot_rows = iota((Q * TA, 64), 0)
    slot_lanes = iota((Q * TA, 64), 1)
    to_slot = jnp.where(
        jnp.logical_and(code_row[0:1, :64] == (slot_rows >> 2),
                        (slot_lanes >> 4) == (slot_rows & 3)), 1.0, 0.0)
    sent = dot_left_exact(to_slot, fluxes)
    for o in range(G):
        flux_out[o] = sent[8 * o:8 * o + 8]
    returned = [
        to_peer(o, flux_out.at[o], flux_in.at[o], flux_send.at[o], flux_recv.at[o])
        for o in range(1, G)
    ]
    for copy in returned:
        copy.start()
    flux_in[0] = flux_out[0]

    lax.fori_loop(first_groups, groups, advect, 0)

    lane8 = lane
    row8 = sub
    where_x = []
    where_y = []
    for o in range(G):
        p0 = req_in[o, 0:1, :].astype(jnp.int32)
        p1 = req_in[o, 1:2, :].astype(jnp.int32)
        place = jnp.where(row8 < TA, p0, p1)
        x0 = (place >> 5) * TA
        where_x.append(jnp.where(lane8 == x0 + (row8 & 3), 1.0, 0.0))
        where_y.append((lane8 >> 2) == (place & 31))
    across = jnp.concatenate(where_x, axis=0).T
    for copy in returned:
        copy.wait_recv()
    values = jnp.concatenate(
        [jnp.where(where_y[o], flux_in[o], 0.0) for o in range(G)], axis=0)
    field_ref[...] = dot_left_exact(across, values)[:BX]

    for copy in requests + winds + halos + replies + returned:
        copy.wait_send()

    def finish_tile(t, carry):
        level_store(t).wait()
        fuel_store(t).wait()
        return carry

    lax.fori_loop(0, TPD, finish_tile, 0)

    def finish_group(zz, carry):
        store(zz).wait()
        return carry

    lax.fori_loop(0, groups, finish_group, 0)


def body(G, H, theta, wind_u, wind_v, level_set, fuel_load, spread_base, tile_owner, tile_place):
    LZ = theta.shape[0]
    assert theta.shape[1:] == (BX, BY) and level_set.shape[2:] == (TPD, S, S)
    anywhere = pl.BlockSpec(memory_space=pl.ANY)
    scalars = pl.BlockSpec(memory_space=pltpu.SMEM)
    vmem = pl.BlockSpec(memory_space=pltpu.VMEM)
    dma = pltpu.SemaphoreType.DMA
    scratch = [
        pltpu.VMEM((LZ, BX + 16, BY), F32),
        pltpu.VMEM((LZ, BX, BY), F32),
        pltpu.VMEM((LZ, BX, BY), F32),
        pltpu.VMEM((LZ, BX, BY), F32),
        pltpu.VMEM((TPD, S + 16, S), F32),
        pltpu.VMEM((2, S + 16, S), F32),
        pltpu.VMEM((TPD, S, S), F32),
        pltpu.VMEM((TPD, S, S), F32),
        pltpu.VMEM((TPD, S, S), F32),
        pltpu.VMEM((2, 2 * S, S), F32),
        pltpu.VMEM((2 * S, 48), BF16),
        pltpu.VMEM((TPD, 48, S), BF16),
        pltpu.VMEM((TA, TPD, S), F32),
        pltpu.VMEM((TPD, 128), jnp.int32),
        pltpu.VMEM((G, 4, 128), F32),
        pltpu.VMEM((G, 4, 128), F32),
        pltpu.VMEM((G, 2, 128), F32),
        pltpu.VMEM((G, 2, 128), F32),
        pltpu.VMEM((G, 8, 128), F32),
        pltpu.VMEM((G, 8, 128), F32),
        pltpu.VMEM((8, 128), F32),
        pltpu.VMEM((6, 8, 128), F32),
        pltpu.VMEM((LZ, 128), F32),
        pltpu.VMEM((2, LZ, 128), F32),
        pltpu.VMEM((2, LZ, 128), F32),
        pltpu.VMEM((2, LZ, 128), F32),
        dma((8,)), dma((TPD,)), dma((TPD,)), dma((LZ // GROUP,)),
        dma((G,)), dma((G,)), dma((G,)), dma((G,)), dma((G,)), dma((G,)),
        dma((6,)), dma((6,)), dma((4,)), dma((4,)),
    ]
    part, level_next, fuel_next, field = pl.pallas_call(
        functools.partial(kernel, G, H, LZ),
        out_shape=(
            jax.ShapeDtypeStruct(theta.shape, F32),
            jax.ShapeDtypeStruct(level_set.shape, F32),
            jax.ShapeDtypeStruct(level_set.shape, F32),
            jax.ShapeDtypeStruct((BX, BY), F32),
        ),
        in_specs=[anywhere] * 6 + [scalars] * 2,
        out_specs=(anywhere, anywhere, anywhere, vmem),
        scratch_shapes=scratch,
        compiler_params=pltpu.CompilerParams(
            collective_id=0, has_side_effects=True, vmem_limit_bytes=40 * 1024 * 1024),
    )(theta, wind_u, wind_v, level_set, fuel_load, spread_base, tile_owner, tile_place)
    profile = 2.0 * jnp.exp(-(jnp.arange(LZ, dtype=F32) + 0.5) / (LZ / 4.0))
    theta_next = part + field[None, :, :] * profile[:, None, None]
    return (theta_next, level_next, fuel_next)


def solution(mesh):
    columns = P(None, "gx", "gy")
    tiles = P("gx", "gy", None, None, None)
    lists = P("gx", "gy", None)
    return jax.shard_map(
        functools.partial(body, mesh.shape["gx"], mesh.shape["gy"]),
        mesh=mesh,
        in_specs=(columns, columns, columns, tiles, tiles, tiles, lists, lists),
        out_specs=(columns, tiles, tiles),
        check_vma=False,
    )
```

```python
import functools

import jax
import jax.numpy as jnp
from jax import lax
from jax.experimental import pallas as pl
from jax.experimental.pallas import tpu as pltpu
from jax.sharding import PartitionSpec as P

TA = 4
R = 32
KSUB = 6
CAP = 2
TPD = 16
S = 128
BX = 64
BY = 128
GROUP = 8

MESH = pl.DeviceIdType.MESH
F32 = jnp.float32
BF16 = jnp.bfloat16


def iota(shape, dim):
    return lax.broadcasted_iota(jnp.int32, shape, dim)


def pieces(x):
    high = x.astype(BF16)
    rest = x - high.astype(F32)
    middle = rest.astype(BF16)
    low = (rest - middle.astype(F32)).astype(BF16)
    return (high, middle, low)


def dot(a, b):
    return jnp.dot(a, b, preferred_element_type=F32)


def dot_left_exact(a, b):
    a = a.astype(BF16)
    high, middle, low = pieces(b)
    return dot(a, high) + (dot(a, middle) + dot(a, low))


def dot_right_exact(a, b):
    b = b.astype(BF16)
    high, middle, low = pieces(a)
    return dot(high, b) + (dot(middle, b) + dot(low, b))


def interp_weight(fine, column):
    where_fine = (fine.astype(F32) + 0.5) / R + 0.5
    return jnp.maximum(0.0, 1.0 - jnp.abs(where_fine - column.astype(F32)))


def kernel(
    G, H, LZ,
    theta_hbm, u_hbm, v_hbm, level_hbm, fuel_hbm, base_hbm, owner_hbm, place_hbm,
    part_hbm, level_out, fuel_out, field_ref,
    th, uu, vv, part, lev, lout, ping, pong, fin, burn, fout, base, wind, scaled,
    wide, small, rows, code_col, owner_ref, place_ref,
    req_out, req_in, rep_out, rep_in, flux_out, flux_in,
    yw_out, yw_in, yth_out, yth_in, xth_out, xth_in,
    in_sem, lev_sem, fuel_sem, part_sem,
    req_send, req_recv, rep_send, rep_recv, flux_send, flux_recv,
    yw_send, yw_recv, th_send, th_recv,
):
    Q = G * CAP
    i = lax.axis_index("gx")
    j = lax.axis_index("gy")

    def gx(offset):
        return lax.rem(i + (offset % G), G)

    def gy(offset):
        return lax.rem(j + (offset % H), H)

    loads = [
        pltpu.make_async_copy(owner_hbm, owner_ref, in_sem.at[8]),
        pltpu.make_async_copy(place_hbm, place_ref, in_sem.at[9]),
        pltpu.make_async_copy(u_hbm.at[0], uu.at[0], in_sem.at[0]),
        pltpu.make_async_copy(v_hbm.at[0], vv.at[0], in_sem.at[1]),
        pltpu.make_async_copy(theta_hbm, th.at[:, 8:8 + BX, :], in_sem.at[2]),
        pltpu.make_async_copy(u_hbm.at[1:], uu.at[1:], in_sem.at[3]),
        pltpu.make_async_copy(v_hbm.at[1:], vv.at[1:], in_sem.at[4]),
        pltpu.make_async_copy(level_hbm.at[0, 0], lev.at[:, 8:8 + S, :], in_sem.at[5]),
        pltpu.make_async_copy(fuel_hbm.at[0, 0], fin, in_sem.at[6]),
        pltpu.make_async_copy(base_hbm.at[0, 0], base, in_sem.at[7]),
    ]
    for load in loads:
        load.start()

    corners = [(0, 1), (0, -1), (-1, 1), (-1, -1), (1, 1), (1, -1)]
    barrier = pltpu.get_barrier_semaphore()
    for o in range(1, G):
        pl.semaphore_signal(barrier, inc=1, device_id=(gx(o), j), device_id_type=MESH)
    for dx, dy in corners:
        pl.semaphore_signal(barrier, inc=1, device_id=(gx(dx), gy(dy)), device_id_type=MESH)

    loads[0].wait()
    loads[1].wait()
    lane = iota((8, 128), 1)
    lane16 = lane & (TPD - 1)
    sub16 = iota((TPD, 128), 0)
    own_row = jnp.zeros((8, 128), jnp.int32)
    place_row = jnp.zeros((8, 128), jnp.int32)
    own_col = jnp.zeros((TPD, 128), jnp.int32)
    for t in range(TPD):
        own_row = jnp.where(lane16 == t, owner_ref[0, 0, t], own_row)
        place_row = jnp.where(lane16 == t, place_ref[0, 0, t], place_row)
        own_col = jnp.where(sub16 == t, owner_ref[0, 0, t], own_col)
    rank_row = jnp.zeros((8, 128), jnp.int32)
    rank_col = jnp.zeros((TPD, 128), jnp.int32)
    for t in range(TPD):
        rank_row += jnp.where(
            jnp.logical_and(own_row == owner_ref[0, 0, t], lane16 > t), 1, 0)
        rank_col += jnp.where(
            jnp.logical_and(own_col == owner_ref[0, 0, t], sub16 > t), 1, 0)

    def code_of(owner, rank):
        away = owner - i
        return jnp.where(away < 0, away + G, away) * CAP + rank

    code_row = code_of(own_row, rank_row)
    code_col[...] = code_of(own_col, rank_col)

    row1 = code_row[0:1]
    place1 = place_row[0:1]
    wanted = jnp.where(
        jnp.logical_and(row1 == iota((Q, 128), 0), iota((Q, 128), 1) < TPD),
        place1 + 1, 0).astype(F32)
    asked = jnp.broadcast_to(jnp.sum(wanted, axis=1, keepdims=True) - 1.0, (Q, 128))

    loads[2].wait()
    loads[3].wait()
    for o in range(G):
        req_out[o, 0:2, :] = asked[2 * o:2 * o + 2]
        edge = 0 if o == G - 1 else BX - 1
        req_out[o, 2:3, :] = uu[0, edge:edge + 1, :]
        req_out[o, 3:4, :] = vv[0, edge:edge + 1, :]
    packed = jnp.zeros((8, 128), F32)
    for g in range(16):
        source = uu if g < 8 else vv
        cell = source[0, 8 * (g % 8):8 * (g % 8) + 8, :]
        packed = jnp.where((lane >> 1) == g, pltpu.roll(cell, 2 * g + 1, 1), packed)
    yw_out[...] = packed

    pl.semaphore_wait(barrier, G - 1 + len(corners))

    def to_peer(o, out, into, send, recv):
        return pltpu.make_async_remote_copy(
            src_ref=out, dst_ref=into, send_sem=send, recv_sem=recv,
            device_id=(gx(o), j), device_id_type=MESH)

    requests = [
        to_peer(o, req_out.at[o], req_in.at[o], req_send.at[o], req_recv.at[o])
        for o in range(1, G)
    ]
    winds = [
        pltpu.make_async_remote_copy(
            src_ref=yw_out, dst_ref=yw_in.at[n], send_sem=yw_send.at[n],
            recv_sem=yw_recv.at[n], device_id=(gx(dx), gy(dy)), device_id_type=MESH)
        for n, (dx, dy) in enumerate(corners)
    ]
    for copy in requests + winds:
        copy.start()
    req_in[0] = req_out[0]

    fine_of = iota((2 * S, 48), 0)
    slot_of = iota((2 * S, 48), 1) & 15
    column = slot_of - 6 * (fine_of >> 7)
    a3 = jnp.where(
        jnp.logical_and(column >= 0, column < 6),
        interp_weight(fine_of & (S - 1), column), 0.0).astype(BF16)
    wide[...] = a3

    loads[4].wait()

    def pack(zz, carry):
        acc = jnp.zeros((8, 128), F32)
        for zl in range(GROUP):
            z = zz * GROUP + zl
            for g in range(8):
                n = zl * 8 + g
                cell = th[z, 8 + 8 * g:16 + 8 * g, :]
                acc = jnp.where((lane >> 1) == n, pltpu.roll(cell, (2 * n + 1) % 128, 1), acc)
            xth_out[0, pl.ds(z, 1), :] = th[z, 7 + BX:8 + BX, :]
            xth_out[1, pl.ds(z, 1), :] = th[z, 8:9, :]
        yth_out[pl.ds(pl.multiple_of(zz * 8, 8), 8), :] = acc
        return carry

    lax.fori_loop(0, LZ // GROUP, pack, 0)
    halos = []
    for n, (out, into, dx, dy) in enumerate([
        (xth_out.at[0], xth_in.at[0], 1, 0),
        (xth_out.at[1], xth_in.at[1], -1, 0),
        (yth_out, yth_in.at[0], 0, 1),
        (yth_out, yth_in.at[1], 0, -1),
    ]):
        halos.append(pltpu.make_async_remote_copy(
            src_ref=out, dst_ref=into, send_sem=th_send.at[n], recv_sem=th_recv.at[n],
            device_id=(gx(dx), gy(dy)), device_id_type=MESH))
    for copy in halos:
        copy.start()

    for copy in winds:
        copy.wait_recv()
    for copy in requests:
        copy.wait_recv()
    odd = (lane & 1) == 1
    ends = jnp.logical_or(lane == 0, lane == 127)
    is_first = i == 0
    is_last = i == G - 1
    south_ok = jnp.where(j > 0, 1.0, 0.0).astype(F32)
    north_ok = jnp.where(j < H - 1, 1.0, 0.0).astype(F32)
    west_ok = jnp.where(i > 0, 1.0, 0.0).astype(F32)
    east_ok = jnp.where(i < G - 1, 1.0, 0.0).astype(F32)

    def both(south, north):
        return jnp.where(odd, north * north_ok, south * south_ok)

    def unpack(mixed, n):
        return pltpu.roll(mixed, (127 - 2 * n) % 128, 1)

    sub = iota((8, 128), 0)
    here = both(yw_in[0], yw_in[1])
    east = both(yw_in[2], yw_in[3]) * east_ok
    west = both(yw_in[4], yw_in[5]) * west_ok
    surface = []
    for c, source in ((0, uu), (1, vv)):
        zeros = jnp.zeros((8, 128), F32)
        left = [source[0]]
        right = [jnp.where(ends, unpack(here, 8 * c + g), 0.0) for g in range(8)]
        east_row = req_in[G - 1, 2 + c:3 + c, :] * east_ok
        west_row = req_in[1, 2 + c:3 + c, :] * west_ok
        left.append(jnp.where(sub == 0, east_row, 0.0))
        left += [zeros] * 6
        left.append(jnp.where(sub == 7, west_row, 0.0))
        right.append(jnp.where(jnp.logical_and(ends, sub == 0), unpack(east, 8 * c), 0.0))
        right += [zeros] * 6
        right.append(jnp.where(jnp.logical_and(ends, sub == 7), unpack(west, 8 * c + 7), 0.0))
        surface.append(jnp.concatenate(
            [jnp.concatenate(left, axis=0), jnp.concatenate(right, axis=0)], axis=1))

    lane_q = iota((16, 128), 1)
    k_q = iota((16, 128), 0)
    pick = ([], [])
    masks = []
    later = []
    for q in range(Q):
        place = req_in[q // CAP, q % CAP:q % CAP + 1, :].astype(jnp.int32)
        x0 = (place >> 5) * TA
        y0 = (place & 31) * TA
        for c in range(2):
            m = k_q - 6 * c
            hit = jnp.logical_and(
                lane_q == ((x0 - 1 + m) & 127), jnp.logical_and(m >= 0, m < 6))
            pick[c].append(jnp.where(hit, 1.0, 0.0))
        low = (lane_q - (y0 - 1)) & 255
        high = (lane_q + 128 - (y0 - 1)) & 255
        masks.append(jnp.concatenate(
            [jnp.where(low < 6, 1.0, 0.0), jnp.where(high < 6, 1.0, 0.0)], axis=1))
        later.append(jnp.broadcast_to((y0 & 4) != 0, (16, 128)))
    found = (dot_left_exact(jnp.concatenate(pick[0], axis=0), surface[0])
             + dot_left_exact(jnp.concatenate(pick[1], axis=0), surface[1]))
    found = found * jnp.concatenate(masks, axis=0)
    c_e = iota((256, 256), 0)
    l_e = iota((256, 256), 1)
    shift = jnp.where(l_e < 128, 1, 5)
    squeeze = jnp.where(((c_e + shift) & 7) == (l_e & 7), 1.0, 0.0)
    tight = dot_right_exact(found, squeeze)
    own_lanes = (lane_q >> 3) == k_q
    for q in range(Q):
        block = tight[16 * q:16 * q + 16]
        chosen = jnp.where(later[q], block[:, 128:], block[:, :128])
        rep_out[q // CAP, q % CAP:q % CAP + 1, :] = jnp.sum(
            jnp.where(own_lanes, chosen, 0.0), axis=0, keepdims=True)
    replies = [
        to_peer(-o, rep_out.at[o], rep_in.at[o], rep_send.at[o], rep_recv.at[o])
        for o in range(1, G)
    ]
    for copy in replies:
        copy.start()
    rep_in[0] = rep_out[0]

    def advect(zz, carry):
        rows_of = pl.ds(pl.multiple_of(zz * 8, 8), 8)
        mixed = both(yth_in[0, rows_of, :], yth_in[1, rows_of, :])
        for zl in range(GROUP):
            z = zz * GROUP + zl
            for g in range(8):
                at = 8 + 8 * g
                centre = th[z, at:at + 8, :]
                before = th[z, at - 1:at + 7, :]
                after = th[z, at + 1:at + 9, :]
                edge = unpack(mixed, zl * 8 + g)
                south = pltpu.roll(jnp.where(lane == 127, edge, centre), 1, 1)
                north = pltpu.roll(jnp.where(lane == 0, edge, centre), 127, 1)
                u = uu[z, 8 * g:8 * g + 8, :]
                v = vv[z, 8 * g:8 * g + 8, :]
                total = (jnp.maximum(u, 0.0) * (centre - before)
                         + jnp.minimum(u, 0.0) * (after - centre)
                         + jnp.maximum(v, 0.0) * (centre - south)
                         + jnp.minimum(v, 0.0) * (north - centre))
                part[z, 8 * g:8 * g + 8, :] = centre - 0.4 * total
        store(zz).start()
        return carry

    def store(zz):
        levels = pl.ds(zz * GROUP, GROUP)
        return pltpu.make_async_copy(part.at[levels], part_hbm.at[levels], part_sem.at[zz])

    groups = LZ // GROUP
    first_groups = groups // 2
    for copy in halos:
        copy.wait_recv()
    loads[5].wait()
    loads[6].wait()

    def rim(zz, carry):
        for zl in range(GROUP):
            z = zz * GROUP + zl
            th[z, 7:8, :] = xth_in[0, pl.ds(z, 1), :] * west_ok
            th[z, 8 + BX:9 + BX, :] = xth_in[1, pl.ds(z, 1), :] * east_ok
        return carry

    lax.fori_loop(0, groups, rim, 0)
    lax.fori_loop(0, first_groups, advect, 0)

    for copy in replies:
        copy.wait_recv()
    answers = jnp.concatenate([rep_in[o] for o in range(G)], axis=0)
    is_slot = jnp.where(code_col[:, :Q] == iota((TPD, Q), 1), 1.0, 0.0)
    patch = dot_left_exact(is_slot, answers)
    spread = jnp.concatenate(
        [jnp.where(own_lanes, patch[t:t + 1], 0.0) for t in range(TPD)], axis=0)
    by_y = jnp.where(
        (iota((128, 128), 0) & 7) < 6,
        interp_weight(iota((128, 128), 1), iota((128, 128), 0) & 7), 0.0)
    along_y = dot_right_exact(spread, by_y)
    high, middle, low = pieces(along_y)
    for t in range(TPD):
        small[t, 0:16, :] = high[16 * t:16 * t + 16]
        small[t, 16:32, :] = middle[16 * t:16 * t + 16]
        small[t, 32:48, :] = low[16 * t:16 * t + 16]

    for load in loads[7:]:
        load.wait()
    pair = 2
    lane_c = iota((R, 128), 1)
    first_lane = lane_c == 0
    last_lane = lane_c == 127

    def level_store(t):
        return pltpu.make_async_copy(lout.at[t], level_out.at[0, 0, t], lev_sem.at[t])

    def fuel_store(t):
        return pltpu.make_async_copy(fout.at[t], fuel_out.at[0, 0, t], fuel_sem.at[t])

    def pad_tile(t, carry):
        lev[t, 7:8, :] = lev[t, 8:9, :]
        lev[t, 8 + S:9 + S, :] = lev[t, 7 + S:8 + S, :]
        return carry

    lax.fori_loop(0, TPD, pad_tile, 0)

    def fire(step, carry):
        for p in range(pair):
            t = step * pair + p
            wind[p] = dot(wide[...], small[t])
            for b in range(S // R):
                strength = 0.015 * base[t, R * b:R * b + R, :]
                scaled[p, R * b:R * b + R, :] = strength
                wind[p, R * b:R * b + R, :] = wind[p, R * b:R * b + R, :] * strength
                wind[p, S + R * b:S + R * b + R, :] = (
                    wind[p, S + R * b:S + R * b + R, :] * strength)
        for k in range(KSUB):
            last = k == KSUB - 1
            for p in range(pair):
                t = step * pair + p
                old = lev.at[t] if k == 0 else (ping, pong)[(k - 1) % 2].at[p]
                new = (ping, pong)[k % 2].at[p]
                fuel_old = fin.at[t] if k == 0 else burn.at[p]
                for b in range(S // R):
                    at = 8 + R * b
                    here_b = slice(R * b, R * b + R)
                    centre = old[at:at + R, :]
                    before = old[at - 1:at - 1 + R, :]
                    after = old[at + 1:at + 1 + R, :]
                    left = jnp.where(first_lane, centre, pltpu.roll(centre, 1, 1))
                    right = jnp.where(last_lane, centre, pltpu.roll(centre, 127, 1))
                    dx = after - before
                    dy = right - left
                    around = (after + before) + (right + left)
                    square = (dx * dx + 0.04) + dy * dy
                    length = square * lax.rsqrt(square)
                    blown = (wind[p, R * b:R * b + R, :] * dx
                             + wind[p, S + R * b:S + R * b + R, :] * dy)
                    rate = jnp.maximum(scaled[p, here_b, :] * length + blown, 0.0)
                    level = (0.4 * centre + 0.15 * around) - rate
                    fuel = fuel_old[here_b, :] * (0.925 + 0.075 * jnp.tanh(level))
                    if last:
                        lout[t, here_b, :] = level
                        fout[t, here_b, :] = fuel
                        burnt = fin[t, here_b, :] - fuel
                        rows[b, pl.ds(t, 1), :] = jnp.sum(burnt, axis=0, keepdims=True)
                    else:
                        new[at:at + R, :] = level
                        if b == 0:
                            new[7:8, :] = level[0:1]
                        if b == S // R - 1:
                            new[8 + S:9 + S, :] = level[R - 1:R]
                        burn[p, here_b, :] = fuel
        for p in range(pair):
            t = step * pair + p
            level_store(t).start()
            fuel_store(t).start()
        return carry

    lax.fori_loop(0, TPD // pair, fire, 0)

    l_m = iota((128, 128), 0)
    c_m = iota((128, 128), 1)
    mean = jnp.where((l_m >> 5) == (c_m & 3), 1.0 / (R * R), 0.0)
    fluxes = dot_right_exact(jnp.concatenate([rows[b] for b in range(TA)], axis=0), mean)
    slot_rows = iota((Q * TA, 64), 0)
    slot_lanes = iota((Q * TA, 64), 1)
    to_slot = jnp.where(
        jnp.logical_and(code_row[0:1, :64] == (slot_rows >> 2),
                        (slot_lanes >> 4) == (slot_rows & 3)), 1.0, 0.0)
    sent = dot_left_exact(to_slot, fluxes)
    for o in range(G):
        flux_out[o] = sent[8 * o:8 * o + 8]
    returned = [
        to_peer(o, flux_out.at[o], flux_in.at[o], flux_send.at[o], flux_recv.at[o])
        for o in range(1, G)
    ]
    for copy in returned:
        copy.start()
    flux_in[0] = flux_out[0]

    lax.fori_loop(first_groups, groups, advect, 0)

    lane8 = lane
    row8 = sub
    where_x = []
    where_y = []
    for o in range(G):
        p0 = req_in[o, 0:1, :].astype(jnp.int32)
        p1 = req_in[o, 1:2, :].astype(jnp.int32)
        place = jnp.where(row8 < TA, p0, p1)
        x0 = (place >> 5) * TA
        where_x.append(jnp.where(lane8 == x0 + (row8 & 3), 1.0, 0.0))
        where_y.append((lane8 >> 2) == (place & 31))
    across = jnp.concatenate(where_x, axis=0).T
    for copy in returned:
        copy.wait_recv()
    values = jnp.concatenate(
        [jnp.where(where_y[o], flux_in[o], 0.0) for o in range(G)], axis=0)
    field_ref[...] = dot_left_exact(across, values)[:BX]

    for copy in requests + winds + halos + replies + returned:
        copy.wait_send()

    def finish_tile(t, carry):
        level_store(t).wait()
        fuel_store(t).wait()
        return carry

    lax.fori_loop(0, TPD, finish_tile, 0)

    def finish_group(zz, carry):
        store(zz).wait()
        return carry

    lax.fori_loop(0, groups, finish_group, 0)


def finish(LZ, per_step, part, level, fuel, field, theta_next, level_next, fuel_next):
    first = pl.program_id(0) * per_step
    heat = 2.0 * field[...]
    for n in range(per_step):
        z = jnp.full((8, BY), first + n, jnp.int32).astype(F32)
        profile = jnp.exp(-(z + 0.5) / (LZ / 4.0))
        for g in range(BX // 8):
            at = slice(8 * g, 8 * g + 8)
            theta_next[n, at, :] = part[n, at, :] + heat[at] * profile
    level_next[...] = level[...]
    fuel_next[...] = fuel[...]


def body(G, H, theta, wind_u, wind_v, level_set, fuel_load, spread_base, tile_owner, tile_place):
    LZ = theta.shape[0]
    assert theta.shape[1:] == (BX, BY) and level_set.shape[2:] == (TPD, S, S)
    anywhere = pl.BlockSpec(memory_space=pl.ANY)
    far = pl.BlockSpec(memory_space=pltpu.HBM)
    vmem = pl.BlockSpec(memory_space=pltpu.VMEM)
    dma = pltpu.SemaphoreType.DMA
    scratch = [
        pltpu.VMEM((LZ, BX + 16, BY), F32),
        pltpu.VMEM((LZ, BX, BY), F32),
        pltpu.VMEM((LZ, BX, BY), F32),
        pltpu.VMEM((LZ, BX, BY), F32),
        pltpu.VMEM((TPD, S + 16, S), F32),
        pltpu.VMEM((TPD, S, S), F32),
        pltpu.VMEM((2, S + 16, S), F32),
        pltpu.VMEM((2, S + 16, S), F32),
        pltpu.VMEM((TPD, S, S), F32),
        pltpu.VMEM((2, S, S), F32),
        pltpu.VMEM((TPD, S, S), F32),
        pltpu.VMEM((TPD, S, S), F32),
        pltpu.VMEM((2, 2 * S, S), F32),
        pltpu.VMEM((2, S, S), F32),
        pltpu.VMEM((2 * S, 48), BF16),
        pltpu.VMEM((TPD, 48, S), BF16),
        pltpu.VMEM((TA, TPD, S), F32),
        pltpu.VMEM((TPD, 128), jnp.int32),
        pltpu.SMEM((1, 1, TPD), jnp.int32),
        pltpu.SMEM((1, 1, TPD), jnp.int32),
        pltpu.VMEM((G, 4, 128), F32),
        pltpu.VMEM((G, 4, 128), F32),
        pltpu.VMEM((G, 2, 128), F32),
        pltpu.VMEM((G, 2, 128), F32),
        pltpu.VMEM((G, 8, 128), F32),
        pltpu.VMEM((G, 8, 128), F32),
        pltpu.VMEM((8, 128), F32),
        pltpu.VMEM((6, 8, 128), F32),
        pltpu.VMEM((LZ, 128), F32),
        pltpu.VMEM((2, LZ, 128), F32),
        pltpu.VMEM((2, LZ, 128), F32),
        pltpu.VMEM((2, LZ, 128), F32),
        dma((10,)), dma((TPD,)), dma((TPD,)), dma((LZ // GROUP,)),
        dma((G,)), dma((G,)), dma((G,)), dma((G,)), dma((G,)), dma((G,)),
        dma((6,)), dma((6,)), dma((4,)), dma((4,)),
    ]
    part, level_next, fuel_next, field = pl.pallas_call(
        functools.partial(kernel, G, H, LZ),
        out_shape=(
            jax.ShapeDtypeStruct(theta.shape, F32),
            jax.ShapeDtypeStruct(level_set.shape, F32),
            jax.ShapeDtypeStruct(level_set.shape, F32),
            jax.ShapeDtypeStruct((BX, BY), F32),
        ),
        in_specs=[far] * 8,
        out_specs=(anywhere, anywhere, anywhere, vmem),
        scratch_shapes=scratch,
        compiler_params=pltpu.CompilerParams(
            collective_id=0, has_side_effects=True, vmem_limit_bytes=58 * 1024 * 1024),
    )(theta, wind_u, wind_v, level_set, fuel_load, spread_base, tile_owner, tile_place)
    steps = 8
    levels = pl.BlockSpec((LZ // steps, BX, BY), lambda n: (n, 0, 0))
    two = pl.BlockSpec((1, 1, TPD // steps, S, S), lambda n: (0, 0, n, 0, 0))
    whole = pl.BlockSpec((BX, BY), lambda n: (0, 0))
    return pl.pallas_call(
        functools.partial(finish, LZ, LZ // steps),
        grid=(steps,),
        out_shape=(
            jax.ShapeDtypeStruct(theta.shape, F32),
            jax.ShapeDtypeStruct(level_set.shape, F32),
            jax.ShapeDtypeStruct(level_set.shape, F32),
        ),
        in_specs=[levels, two, two, whole],
        out_specs=(levels, two, two),
        compiler_params=pltpu.CompilerParams(vmem_limit_bytes=58 * 1024 * 1024),
    )(part, level_next, fuel_next, field)


def solution(mesh):
    columns = P(None, "gx", "gy")
    tiles = P("gx", "gy", None, None, None)
    lists = P("gx", "gy", None)
    return jax.shard_map(
        functools.partial(body, mesh.shape["gx"], mesh.shape["gy"]),
        mesh=mesh,
        in_specs=(columns, columns, columns, tiles, tiles, tiles, lists, lists),
        out_specs=(columns, tiles, tiles),
        check_vma=False,
    )
```

```python
import functools

import jax
import jax.numpy as jnp
from jax import lax
from jax.experimental import pallas as pl
from jax.experimental.pallas import tpu as pltpu
from jax.sharding import PartitionSpec as P

TA = 4
R = 32
KSUB = 6
CAP = 2
TPD = 16
S = 128
BX = 64
BY = 128
GROUP = 8
PAIR = 2
LIMITS = (48, 24, 24)

MESH = pl.DeviceIdType.MESH
F32 = jnp.float32
BF16 = jnp.bfloat16


def iota(shape, dim):
    return lax.broadcasted_iota(jnp.int32, shape, dim)


def pieces(x):
    high = x.astype(BF16)
    rest = x - high.astype(F32)
    middle = rest.astype(BF16)
    low = (rest - middle.astype(F32)).astype(BF16)
    return (high, middle, low)


def dot(a, b):
    return jnp.dot(a, b, preferred_element_type=F32)


def dot_left_exact(a, b):
    a = a.astype(BF16)
    high, middle, low = pieces(b)
    return dot(a, high) + (dot(a, middle) + dot(a, low))


def dot_right_exact(a, b):
    b = b.astype(BF16)
    high, middle, low = pieces(a)
    return dot(high, b) + (dot(middle, b) + dot(low, b))


def interp_weight(fine, column):
    where_fine = (fine.astype(F32) + 0.5) / R + 0.5
    return jnp.maximum(0.0, 1.0 - jnp.abs(where_fine - column.astype(F32)))


def exchange(
    G, H, LZ,
    theta_hbm, u_hbm, v_hbm, owner_hbm, place_hbm,
    small, code_out, asked_out, ymix, xhalo,
    th, u_low, v_low, code_col, owner_ref, place_ref,
    req_out, req_in, rep_out, rep_in,
    yw_out, yw_in, yth_out, yth_in, xth_out, xth_in,
    in_sem,
    req_send, req_recv, rep_send, rep_recv,
    yw_send, yw_recv, th_send, th_recv,
):
    Q = G * CAP
    i = lax.axis_index("gx")
    j = lax.axis_index("gy")

    def gx(offset):
        return lax.rem(i + (offset % G), G)

    def gy(offset):
        return lax.rem(j + (offset % H), H)

    loads = [
        pltpu.make_async_copy(owner_hbm, owner_ref, in_sem.at[0]),
        pltpu.make_async_copy(place_hbm, place_ref, in_sem.at[1]),
        pltpu.make_async_copy(u_hbm.at[0], u_low, in_sem.at[2]),
        pltpu.make_async_copy(v_hbm.at[0], v_low, in_sem.at[3]),
        pltpu.make_async_copy(theta_hbm, th, in_sem.at[4]),
    ]
    for load in loads:
        load.start()

    corners = [(0, 1), (0, -1), (-1, 1), (-1, -1), (1, 1), (1, -1)]
    barrier = pltpu.get_barrier_semaphore()
    for o in range(1, G):
        pl.semaphore_signal(barrier, inc=1, device_id=(gx(o), j), device_id_type=MESH)
    for dx, dy in corners:
        pl.semaphore_signal(barrier, inc=1, device_id=(gx(dx), gy(dy)), device_id_type=MESH)

    loads[0].wait()
    loads[1].wait()
    lane = iota((8, 128), 1)
    lane16 = lane & (TPD - 1)
    sub16 = iota((TPD, 128), 0)
    own_row = jnp.zeros((8, 128), jnp.int32)
    place_row = jnp.zeros((8, 128), jnp.int32)
    own_col = jnp.zeros((TPD, 128), jnp.int32)
    for t in range(TPD):
        own_row = jnp.where(lane16 == t, owner_ref[0, 0, t], own_row)
        place_row = jnp.where(lane16 == t, place_ref[0, 0, t], place_row)
        own_col = jnp.where(sub16 == t, owner_ref[0, 0, t], own_col)
    rank_row = jnp.zeros((8, 128), jnp.int32)
    rank_col = jnp.zeros((TPD, 128), jnp.int32)
    for t in range(TPD):
        rank_row += jnp.where(
            jnp.logical_and(own_row == owner_ref[0, 0, t], lane16 > t), 1, 0)
        rank_col += jnp.where(
            jnp.logical_and(own_col == owner_ref[0, 0, t], sub16 > t), 1, 0)

    def code_of(owner, rank):
        away = owner - i
        return jnp.where(away < 0, away + G, away) * CAP + rank

    code_row = code_of(own_row, rank_row)
    code_out[...] = code_row
    code_col[...] = code_of(own_col, rank_col)

    row1 = code_row[0:1]
    place1 = place_row[0:1]
    wanted = jnp.where(
        jnp.logical_and(row1 == iota((Q, 128), 0), iota((Q, 128), 1) < TPD),
        place1 + 1, 0).astype(F32)
    asked = jnp.broadcast_to(jnp.sum(wanted, axis=1, keepdims=True) - 1.0, (Q, 128))

    loads[2].wait()
    loads[3].wait()
    for o in range(G):
        req_out[o, 0:2, :] = asked[2 * o:2 * o + 2]
        edge = 0 if o == G - 1 else BX - 1
        req_out[o, 2:3, :] = u_low[edge:edge + 1, :]
        req_out[o, 3:4, :] = v_low[edge:edge + 1, :]
    packed = jnp.zeros((8, 128), F32)
    for g in range(16):
        source = u_low if g < 8 else v_low
        cell = source[8 * (g % 8):8 * (g % 8) + 8, :]
        packed = jnp.where((lane >> 1) == g, pltpu.roll(cell, 2 * g + 1, 1), packed)
    yw_out[...] = packed

    pl.semaphore_wait(barrier, G - 1 + len(corners))

    def to_peer(o, out, into, send, recv):
        return pltpu.make_async_remote_copy(
            src_ref=out, dst_ref=into, send_sem=send, recv_sem=recv,
            device_id=(gx(o), j), device_id_type=MESH)

    requests = [
        to_peer(o, req_out.at[o], req_in.at[o], req_send.at[o], req_recv.at[o])
        for o in range(1, G)
    ]
    winds = [
        pltpu.make_async_remote_copy(
            src_ref=yw_out, dst_ref=yw_in.at[n], send_sem=yw_send.at[n],
            recv_sem=yw_recv.at[n], device_id=(gx(dx), gy(dy)), device_id_type=MESH)
        for n, (dx, dy) in enumerate(corners)
    ]
    for copy in requests + winds:
        copy.start()
    req_in[0] = req_out[0]

    loads[4].wait()

    def pack(zz, carry):
        acc = jnp.zeros((8, 128), F32)
        for zl in range(GROUP):
            z = zz * GROUP + zl
            for g in range(8):
                n = zl * 8 + g
                cell = th[z, 8 * g:8 * g + 8, :]
                acc = jnp.where((lane >> 1) == n, pltpu.roll(cell, (2 * n + 1) % 128, 1), acc)
            xth_out[0, pl.ds(z, 1), :] = th[z, BX - 1:BX, :]
            xth_out[1, pl.ds(z, 1), :] = th[z, 0:1, :]
        yth_out[pl.ds(pl.multiple_of(zz * 8, 8), 8), :] = acc
        return carry

    lax.fori_loop(0, LZ // GROUP, pack, 0)
    halos = []
    for n, (out, into, dx, dy) in enumerate([
        (xth_out.at[0], xth_in.at[0], 1, 0),
        (xth_out.at[1], xth_in.at[1], -1, 0),
        (yth_out, yth_in.at[0], 0, 1),
        (yth_out, yth_in.at[1], 0, -1),
    ]):
        halos.append(pltpu.make_async_remote_copy(
            src_ref=out, dst_ref=into, send_sem=th_send.at[n], recv_sem=th_recv.at[n],
            device_id=(gx(dx), gy(dy)), device_id_type=MESH))
    for copy in halos:
        copy.start()

    for copy in winds:
        copy.wait_recv()
    for copy in requests:
        copy.wait_recv()
    odd = (lane & 1) == 1
    ends = jnp.logical_or(lane == 0, lane == 127)
    south_ok = jnp.where(j > 0, 1.0, 0.0).astype(F32)
    north_ok = jnp.where(j < H - 1, 1.0, 0.0).astype(F32)
    west_ok = jnp.where(i > 0, 1.0, 0.0).astype(F32)
    east_ok = jnp.where(i < G - 1, 1.0, 0.0).astype(F32)

    def both(south, north):
        return jnp.where(odd, north * north_ok, south * south_ok)

    def unpack(mixed, n):
        return pltpu.roll(mixed, (127 - 2 * n) % 128, 1)

    sub = iota((8, 128), 0)
    here = both(yw_in[0], yw_in[1])
    east = both(yw_in[2], yw_in[3]) * east_ok
    west = both(yw_in[4], yw_in[5]) * west_ok
    surface = []
    for c, source in ((0, u_low), (1, v_low)):
        zeros = jnp.zeros((8, 128), F32)
        left = [source[...]]
        right = [jnp.where(ends, unpack(here, 8 * c + g), 0.0) for g in range(8)]
        east_row = req_in[G - 1, 2 + c:3 + c, :] * east_ok
        west_row = req_in[1, 2 + c:3 + c, :] * west_ok
        left.append(jnp.where(sub == 0, east_row, 0.0))
        left += [zeros] * 6
        left.append(jnp.where(sub == 7, west_row, 0.0))
        right.append(jnp.where(jnp.logical_and(ends, sub == 0), unpack(east, 8 * c), 0.0))
        right += [zeros] * 6
        right.append(jnp.where(jnp.logical_and(ends, sub == 7), unpack(west, 8 * c + 7), 0.0))
        surface.append(jnp.concatenate(
            [jnp.concatenate(left, axis=0), jnp.concatenate(right, axis=0)], axis=1))

    lane_q = iota((16, 128), 1)
    k_q = iota((16, 128), 0)
    pick = ([], [])
    masks = []
    later = []
    for q in range(Q):
        place = req_in[q // CAP, q % CAP:q % CAP + 1, :].astype(jnp.int32)
        x0 = (place >> 5) * TA
        y0 = (place & 31) * TA
        for c in range(2):
            m = k_q - 6 * c
            hit = jnp.logical_and(
                lane_q == ((x0 - 1 + m) & 127), jnp.logical_and(m >= 0, m < 6))
            pick[c].append(jnp.where(hit, 1.0, 0.0))
        low = (lane_q - (y0 - 1)) & 255
        high = (lane_q + 128 - (y0 - 1)) & 255
        masks.append(jnp.concatenate(
            [jnp.where(low < 6, 1.0, 0.0), jnp.where(high < 6, 1.0, 0.0)], axis=1))
        later.append(jnp.broadcast_to((y0 & 4) != 0, (16, 128)))
    found = (dot_left_exact(jnp.concatenate(pick[0], axis=0), surface[0])
             + dot_left_exact(jnp.concatenate(pick[1], axis=0), surface[1]))
    found = found * jnp.concatenate(masks, axis=0)
    c_e = iota((256, 256), 0)
    l_e = iota((256, 256), 1)
    shift = jnp.where(l_e < 128, 1, 5)
    squeeze = jnp.where(((c_e + shift) & 7) == (l_e & 7), 1.0, 0.0)
    tight = dot_right_exact(found, squeeze)
    own_lanes = (lane_q >> 3) == k_q
    for q in range(Q):
        block = tight[16 * q:16 * q + 16]
        chosen = jnp.where(later[q], block[:, 128:], block[:, :128])
        rep_out[q // CAP, q % CAP:q % CAP + 1, :] = jnp.sum(
            jnp.where(own_lanes, chosen, 0.0), axis=0, keepdims=True)
    replies = [
        to_peer(-o, rep_out.at[o], rep_in.at[o], rep_send.at[o], rep_recv.at[o])
        for o in range(1, G)
    ]
    for copy in replies:
        copy.start()
    rep_in[0] = rep_out[0]

    asked_out[...] = req_in[...]
    for copy in halos:
        copy.wait_recv()
    ymix[...] = jnp.where(
        (iota((LZ, 128), 1) & 1) == 1, yth_in[1] * north_ok, yth_in[0] * south_ok)
    xhalo[0] = xth_in[0] * west_ok
    xhalo[1] = xth_in[1] * east_ok

    for copy in replies:
        copy.wait_recv()
    answers = jnp.concatenate([rep_in[o] for o in range(G)], axis=0)
    is_slot = jnp.where(code_col[:, :Q] == iota((TPD, Q), 1), 1.0, 0.0)
    patch = dot_left_exact(is_slot, answers)
    spread = jnp.concatenate(
        [jnp.where(own_lanes, patch[t:t + 1], 0.0) for t in range(TPD)], axis=0)
    by_y = jnp.where(
        (iota((128, 128), 0) & 7) < 6,
        interp_weight(iota((128, 128), 1), iota((128, 128), 0) & 7), 0.0)
    along_y = dot_right_exact(spread, by_y)
    high, middle, low = pieces(along_y)
    for t in range(TPD):
        small[t, 0:16, :] = high[16 * t:16 * t + 16]
        small[t, 16:32, :] = middle[16 * t:16 * t + 16]
        small[t, 32:48, :] = low[16 * t:16 * t + 16]

    for copy in requests + winds + halos + replies:
        copy.wait_send()


def fire(
    small, level_ref, fuel_ref, base, level_out, fuel_out, rows,
    wide, ping, pong, burn, wind, scaled,
):
    step = pl.program_id(0)
    lane_c = iota((R, 128), 1)
    first_lane = lane_c == 0
    last_lane = lane_c == 127

    @pl.when(step == 0)
    def _():
        fine_of = iota((2 * S, 48), 0)
        slot_of = iota((2 * S, 48), 1) & 15
        column = slot_of - 6 * (fine_of >> 7)
        wide[...] = jnp.where(
            jnp.logical_and(column >= 0, column < 6),
            interp_weight(fine_of & (S - 1), column), 0.0).astype(BF16)

    for p in range(PAIR):
        wind[p] = dot(wide[...], small[p])
        pong[p, 8:8 + S, :] = level_ref[0, 0, p]
        pong[p, 7:8, :] = level_ref[0, 0, p, 0:1, :]
        pong[p, 8 + S:9 + S, :] = level_ref[0, 0, p, S - 1:S, :]
        for b in range(S // R):
            strength = 0.015 * base[0, 0, p, R * b:R * b + R, :]
            scaled[p, R * b:R * b + R, :] = strength
            wind[p, R * b:R * b + R, :] = wind[p, R * b:R * b + R, :] * strength
            wind[p, S + R * b:S + R * b + R, :] = (
                wind[p, S + R * b:S + R * b + R, :] * strength)
    for k in range(KSUB):
        last = k == KSUB - 1
        for p in range(PAIR):
            old = (ping, pong)[(k - 1) % 2].at[p]
            new = (ping, pong)[k % 2].at[p]
            fuel_old = fuel_ref.at[0, 0, p] if k == 0 else burn.at[p]
            for b in range(S // R):
                at = 8 + R * b
                here_b = slice(R * b, R * b + R)
                centre = old[at:at + R, :]
                before = old[at - 1:at - 1 + R, :]
                after = old[at + 1:at + 1 + R, :]
                left = jnp.where(first_lane, centre, pltpu.roll(centre, 1, 1))
                right = jnp.where(last_lane, centre, pltpu.roll(centre, 127, 1))
                dx = after - before
                dy = right - left
                around = (after + before) + (right + left)
                square = (dx * dx + 0.04) + dy * dy
                length = square * lax.rsqrt(square)
                blown = (wind[p, R * b:R * b + R, :] * dx
                         + wind[p, S + R * b:S + R * b + R, :] * dy)
                rate = jnp.maximum(scaled[p, here_b, :] * length + blown, 0.0)
                level = (0.4 * centre + 0.15 * around) - rate
                fuel = fuel_old[here_b, :] * (0.925 + 0.075 * jnp.tanh(level))
                if last:
                    level_out[0, 0, p, here_b, :] = level
                    fuel_out[0, 0, p, here_b, :] = fuel
                    burnt = fuel_ref[0, 0, p, here_b, :] - fuel
                    rows[b, pl.ds(step * PAIR + p, 1), :] = jnp.sum(burnt, axis=0, keepdims=True)
                else:
                    new[at:at + R, :] = level
                    if b == 0:
                        new[7:8, :] = level[0:1]
                    if b == S // R - 1:
                        new[8 + S:9 + S, :] = level[R - 1:R]
                    burn[p, here_b, :] = fuel


def gather(
    G, LZ,
    theta_hbm, u_hbm, v_hbm, rows, code_row, req_in, ymix, xhalo,
    part_hbm, field_ref,
    th, uu, vv, part, flux_out, flux_in,
    in_sem, part_sem, flux_send, flux_recv,
):
    Q = G * CAP
    i = lax.axis_index("gx")
    j = lax.axis_index("gy")
    groups = LZ // GROUP
    lane = iota((8, 128), 1)
    sub = iota((8, 128), 0)

    def gx(offset):
        return lax.rem(i + (offset % G), G)

    barrier = pltpu.get_barrier_semaphore()
    for o in range(1, G):
        pl.semaphore_signal(barrier, inc=1, device_id=(gx(o), j), device_id_type=MESH)

    def arrays(zz):
        levels = pl.ds(zz * GROUP, GROUP)
        return [
            pltpu.make_async_copy(
                theta_hbm.at[levels], th.at[levels, 8:8 + BX, :], in_sem.at[0, zz]),
            pltpu.make_async_copy(u_hbm.at[levels], uu.at[levels], in_sem.at[1, zz]),
            pltpu.make_async_copy(v_hbm.at[levels], vv.at[levels], in_sem.at[2, zz]),
        ]

    for zz in range(groups):
        for load in arrays(zz):
            load.start()

    def to_peer(o, out, into, send, recv):
        return pltpu.make_async_remote_copy(
            src_ref=out, dst_ref=into, send_sem=send, recv_sem=recv,
            device_id=(gx(o), j), device_id_type=MESH)

    def unpack(mixed, n):
        return pltpu.roll(mixed, (127 - 2 * n) % 128, 1)

    l_m = iota((128, 128), 0)
    c_m = iota((128, 128), 1)
    mean = jnp.where((l_m >> 5) == (c_m & 3), 1.0 / (R * R), 0.0)
    fluxes = dot_right_exact(jnp.concatenate([rows[b] for b in range(TA)], axis=0), mean)
    slot_rows = iota((Q * TA, 64), 0)
    slot_lanes = iota((Q * TA, 64), 1)
    to_slot = jnp.where(
        jnp.logical_and(code_row[0:1, 0:64] == (slot_rows >> 2),
                        (slot_lanes >> 4) == (slot_rows & 3)), 1.0, 0.0)
    sent = dot_left_exact(to_slot, fluxes)
    for o in range(G):
        flux_out[o] = sent[8 * o:8 * o + 8]
    pl.semaphore_wait(barrier, G - 1)
    returned = [
        to_peer(o, flux_out.at[o], flux_in.at[o], flux_send.at[o], flux_recv.at[o])
        for o in range(1, G)
    ]
    for copy in returned:
        copy.start()
    flux_in[0] = flux_out[0]

    def advect(zz, carry):
        rows_of = pl.ds(pl.multiple_of(zz * 8, 8), 8)
        for load in arrays(zz):
            load.wait()
        mixed = ymix[rows_of, :]
        for zl in range(GROUP):
            z = zz * GROUP + zl
            th[z, 7:8, :] = xhalo[0, pl.ds(z, 1), :]
            th[z, 8 + BX:9 + BX, :] = xhalo[1, pl.ds(z, 1), :]
        for zl in range(GROUP):
            z = zz * GROUP + zl
            for g in range(8):
                at = 8 + 8 * g
                centre = th[z, at:at + 8, :]
                before = th[z, at - 1:at + 7, :]
                after = th[z, at + 1:at + 9, :]
                edge = unpack(mixed, zl * 8 + g)
                south = pltpu.roll(jnp.where(lane == 127, edge, centre), 1, 1)
                north = pltpu.roll(jnp.where(lane == 0, edge, centre), 127, 1)
                u = uu[z, 8 * g:8 * g + 8, :]
                v = vv[z, 8 * g:8 * g + 8, :]
                total = (jnp.maximum(u, 0.0) * (centre - before)
                         + jnp.minimum(u, 0.0) * (after - centre)
                         + jnp.maximum(v, 0.0) * (centre - south)
                         + jnp.minimum(v, 0.0) * (north - centre))
                part[z, 8 * g:8 * g + 8, :] = centre - 0.4 * total
        store(zz).start()
        return carry

    def store(zz):
        levels = pl.ds(zz * GROUP, GROUP)
        return pltpu.make_async_copy(part.at[levels], part_hbm.at[levels], part_sem.at[zz])

    lax.fori_loop(0, groups, advect, 0)

    lane8 = lane
    row8 = sub
    where_x = []
    where_y = []
    for o in range(G):
        p0 = req_in[o, 0:1, :].astype(jnp.int32)
        p1 = req_in[o, 1:2, :].astype(jnp.int32)
        place = jnp.where(row8 < TA, p0, p1)
        x0 = (place >> 5) * TA
        where_x.append(jnp.where(lane8 == x0 + (row8 & 3), 1.0, 0.0))
        where_y.append((lane8 >> 2) == (place & 31))
    across = jnp.concatenate(where_x, axis=0).T
    for copy in returned:
        copy.wait_recv()
    values = jnp.concatenate(
        [jnp.where(where_y[o], flux_in[o], 0.0) for o in range(G)], axis=0)
    field_ref[...] = dot_left_exact(across, values)[:BX]

    for copy in returned:
        copy.wait_send()

    def finish_group(zz, carry):
        store(zz).wait()
        return carry

    lax.fori_loop(0, groups, finish_group, 0)


def body(G, H, theta, wind_u, wind_v, level_set, fuel_load, spread_base, tile_owner, tile_place):
    LZ = theta.shape[0]
    assert theta.shape[1:] == (BX, BY) and level_set.shape[2:] == (TPD, S, S)
    far = pl.BlockSpec(memory_space=pl.ANY)
    vmem = pl.BlockSpec(memory_space=pltpu.VMEM)
    dma = pltpu.SemaphoreType.DMA
    shape = jax.ShapeDtypeStruct
    small, code, asked, ymix, xhalo = pl.pallas_call(
        functools.partial(exchange, G, H, LZ),
        out_shape=(
            shape((TPD, 48, S), BF16),
            shape((8, 128), jnp.int32),
            shape((G, 4, 128), F32),
            shape((LZ, 128), F32),
            shape((2, LZ, 128), F32),
        ),
        in_specs=[far] * 5,
        out_specs=(vmem,) * 5,
        scratch_shapes=[
            pltpu.VMEM((LZ, BX, BY), F32),
            pltpu.VMEM((BX, BY), F32),
            pltpu.VMEM((BX, BY), F32),
            pltpu.VMEM((TPD, 128), jnp.int32),
            pltpu.SMEM((1, 1, TPD), jnp.int32),
            pltpu.SMEM((1, 1, TPD), jnp.int32),
            pltpu.VMEM((G, 4, 128), F32),
            pltpu.VMEM((G, 4, 128), F32),
            pltpu.VMEM((G, 2, 128), F32),
            pltpu.VMEM((G, 2, 128), F32),
            pltpu.VMEM((8, 128), F32),
            pltpu.VMEM((6, 8, 128), F32),
            pltpu.VMEM((LZ, 128), F32),
            pltpu.VMEM((2, LZ, 128), F32),
            pltpu.VMEM((2, LZ, 128), F32),
            pltpu.VMEM((2, LZ, 128), F32),
            dma((5,)),
            dma((G,)), dma((G,)), dma((G,)), dma((G,)),
            dma((6,)), dma((6,)), dma((4,)), dma((4,)),
        ],
        compiler_params=pltpu.CompilerParams(
            collective_id=0, has_side_effects=True, vmem_limit_bytes=LIMITS[0] * 1024 * 1024),
    )(theta, wind_u, wind_v, tile_owner, tile_place)

    steps = TPD // PAIR
    tiles = pl.BlockSpec((1, 1, PAIR, S, S), lambda n: (0, 0, n, 0, 0))
    level_next, fuel_next, rows = pl.pallas_call(
        fire,
        grid=(steps,),
        out_shape=(
            shape(level_set.shape, F32),
            shape(level_set.shape, F32),
            shape((TA, TPD, S), F32),
        ),
        in_specs=[pl.BlockSpec((PAIR, 48, S), lambda n: (n, 0, 0)), tiles, tiles, tiles],
        out_specs=(tiles, tiles, pl.BlockSpec((TA, TPD, S), lambda n: (0, 0, 0))),
        scratch_shapes=[
            pltpu.VMEM((2 * S, 48), BF16),
            pltpu.VMEM((PAIR, S + 16, S), F32),
            pltpu.VMEM((PAIR, S + 16, S), F32),
            pltpu.VMEM((PAIR, S, S), F32),
            pltpu.VMEM((PAIR, 2 * S, S), F32),
            pltpu.VMEM((PAIR, S, S), F32),
        ],
        compiler_params=pltpu.CompilerParams(vmem_limit_bytes=LIMITS[1] * 1024 * 1024),
    )(small, level_set, fuel_load, spread_base)

    groups = LZ // GROUP
    part, field = pl.pallas_call(
        functools.partial(gather, G, LZ),
        out_shape=(shape(theta.shape, F32), shape((BX, BY), F32)),
        in_specs=[far] * 3 + [vmem] * 5,
        out_specs=(far, vmem),
        scratch_shapes=[
            pltpu.VMEM((LZ, BX + 16, BY), F32),
            pltpu.VMEM((LZ, BX, BY), F32),
            pltpu.VMEM((LZ, BX, BY), F32),
            pltpu.VMEM((LZ, BX, BY), F32),
            pltpu.VMEM((G, 8, 128), F32),
            pltpu.VMEM((G, 8, 128), F32),
            dma((3, groups)), dma((groups,)), dma((G,)), dma((G,)),
        ],
        compiler_params=pltpu.CompilerParams(
            collective_id=1, has_side_effects=True, vmem_limit_bytes=LIMITS[2] * 1024 * 1024),
    )(theta, wind_u, wind_v, rows, code, asked, ymix, xhalo)
    profile = 2.0 * jnp.exp(-(jnp.arange(LZ, dtype=F32) + 0.5) / (LZ / 4.0))
    theta_next = part + field[None, :, :] * profile[:, None, None]
    return (theta_next, level_next, fuel_next)


def solution(mesh):
    columns = P(None, "gx", "gy")
    tiles = P("gx", "gy", None, None, None)
    lists = P("gx", "gy", None)
    return jax.shard_map(
        functools.partial(body, mesh.shape["gx"], mesh.shape["gy"]),
        mesh=mesh,
        in_specs=(columns, columns, columns, tiles, tiles, tiles, lists, lists),
        out_specs=(columns, tiles, tiles),
        check_vma=False,
    )
```

```python
import functools

import jax
import jax.numpy as jnp
from jax import lax
from jax.experimental import pallas as pl
from jax.experimental.pallas import tpu as pltpu
from jax.sharding import PartitionSpec as P

TA = 4
R = 32
KSUB = 6
CAP = 2
TPD = 16
S = 128
BX = 64
BY = 128
GROUP = 8

MESH = pl.DeviceIdType.MESH
F32 = jnp.float32
BF16 = jnp.bfloat16


def iota(shape, dim):
    return lax.broadcasted_iota(jnp.int32, shape, dim)


def pieces(x):
    high = x.astype(BF16)
    rest = x - high.astype(F32)
    middle = rest.astype(BF16)
    low = (rest - middle.astype(F32)).astype(BF16)
    return (high, middle, low)


def dot(a, b):
    return jnp.dot(a, b, preferred_element_type=F32)


def dot_left_exact(a, b):
    a = a.astype(BF16)
    high, middle, low = pieces(b)
    return dot(a, high) + (dot(a, middle) + dot(a, low))


def dot_right_exact(a, b):
    b = b.astype(BF16)
    high, middle, low = pieces(a)
    return dot(high, b) + (dot(middle, b) + dot(low, b))


def interp_weight(fine, column):
    where_fine = (fine.astype(F32) + 0.5) / R + 0.5
    return jnp.maximum(0.0, 1.0 - jnp.abs(where_fine - column.astype(F32)))


def kernel(
    G, H, LZ,
    theta_hbm, u_hbm, v_hbm, level_hbm, fuel_hbm, base_hbm, lists_hbm,
    part_hbm, level_out, fuel_out, field_ref,
    th, uu, vv, part, lev, lout, ping, pong, fin, burn, fout, base, wind, scaled,
    wide, small, rows, code_col, lists,
    req_out, req_in, rep_out, rep_in, flux_out, flux_in,
    yw_out, yw_in, yth_out, yth_in, xth_out, xth_in,
    in_sem, lev_sem, fuel_sem, part_sem,
    req_send, req_recv, rep_send, rep_recv, flux_send, flux_recv,
    yw_send, yw_recv, th_send, th_recv,
):
    Q = G * CAP
    i = lax.axis_index("gx")
    j = lax.axis_index("gy")

    def gx(offset):
        return lax.rem(i + (offset % G), G)

    def gy(offset):
        return lax.rem(j + (offset % H), H)

    loads = [
        pltpu.make_async_copy(lists_hbm, lists, in_sem.at[8]),
        pltpu.make_async_copy(u_hbm.at[0], uu.at[0], in_sem.at[0]),
        pltpu.make_async_copy(v_hbm.at[0], vv.at[0], in_sem.at[1]),
        pltpu.make_async_copy(theta_hbm, th.at[:, 8:8 + BX, :], in_sem.at[2]),
        pltpu.make_async_copy(u_hbm.at[1:], uu.at[1:], in_sem.at[3]),
        pltpu.make_async_copy(v_hbm.at[1:], vv.at[1:], in_sem.at[4]),
        pltpu.make_async_copy(level_hbm.at[0, 0], lev.at[:, 8:8 + S, :], in_sem.at[5]),
        pltpu.make_async_copy(fuel_hbm.at[0, 0], fin, in_sem.at[6]),
        pltpu.make_async_copy(base_hbm.at[0, 0], base, in_sem.at[7]),
    ]
    for load in loads:
        load.start()

    corners = [(0, 1), (0, -1), (-1, 1), (-1, -1), (1, 1), (1, -1)]
    barrier = pltpu.get_barrier_semaphore()
    for o in range(1, G):
        pl.semaphore_signal(barrier, inc=1, device_id=(gx(o), j), device_id_type=MESH)
    for dx, dy in corners:
        pl.semaphore_signal(barrier, inc=1, device_id=(gx(dx), gy(dy)), device_id_type=MESH)

    loads[0].wait()
    lane = iota((8, 128), 1)
    lane16 = lane & (TPD - 1)
    sub16 = iota((TPD, 128), 0)
    own_row = jnp.zeros((8, 128), jnp.int32)
    place_row = jnp.zeros((8, 128), jnp.int32)
    own_col = jnp.zeros((TPD, 128), jnp.int32)
    for t in range(TPD):
        own_row = jnp.where(lane16 == t, lists[0, 0, t], own_row)
        place_row = jnp.where(lane16 == t, lists[0, 1, t], place_row)
        own_col = jnp.where(sub16 == t, lists[0, 0, t], own_col)
    rank_row = jnp.zeros((8, 128), jnp.int32)
    rank_col = jnp.zeros((TPD, 128), jnp.int32)
    for t in range(TPD):
        rank_row += jnp.where(
            jnp.logical_and(own_row == lists[0, 0, t], lane16 > t), 1, 0)
        rank_col += jnp.where(
            jnp.logical_and(own_col == lists[0, 0, t], sub16 > t), 1, 0)

    def code_of(owner, rank):
        away = owner - i
        return jnp.where(away < 0, away + G, away) * CAP + rank

    code_row = code_of(own_row, rank_row)
    code_col[...] = code_of(own_col, rank_col)

    row1 = code_row[0:1]
    place1 = place_row[0:1]
    wanted = jnp.where(
        jnp.logical_and(row1 == iota((Q, 128), 0), iota((Q, 128), 1) < TPD),
        place1 + 1, 0).astype(F32)
    asked = jnp.broadcast_to(jnp.sum(wanted, axis=1, keepdims=True) - 1.0, (Q, 128))

    loads[1].wait()
    loads[2].wait()
    for o in range(G):
        req_out[o, 0:2, :] = asked[2 * o:2 * o + 2]
        edge = 0 if o == G - 1 else BX - 1
        req_out[o, 2:3, :] = uu[0, edge:edge + 1, :]
        req_out[o, 3:4, :] = vv[0, edge:edge + 1, :]
    packed = jnp.zeros((8, 128), F32)
    for g in range(16):
        source = uu if g < 8 else vv
        cell = source[0, 8 * (g % 8):8 * (g % 8) + 8, :]
        packed = jnp.where((lane >> 1) == g, pltpu.roll(cell, 2 * g + 1, 1), packed)
    yw_out[...] = packed

    pl.semaphore_wait(barrier, G - 1 + len(corners))

    def to_peer(o, out, into, send, recv):
        return pltpu.make_async_remote_copy(
            src_ref=out, dst_ref=into, send_sem=send, recv_sem=recv,
            device_id=(gx(o), j), device_id_type=MESH)

    requests = [
        to_peer(o, req_out.at[o], req_in.at[o], req_send.at[o], req_recv.at[o])
        for o in range(1, G)
    ]
    winds = [
        pltpu.make_async_remote_copy(
            src_ref=yw_out, dst_ref=yw_in.at[n], send_sem=yw_send.at[n],
            recv_sem=yw_recv.at[n], device_id=(gx(dx), gy(dy)), device_id_type=MESH)
        for n, (dx, dy) in enumerate(corners)
    ]
    for copy in requests + winds:
        copy.start()
    req_in[0] = req_out[0]

    fine_of = iota((2 * S, 48), 0)
    slot_of = iota((2 * S, 48), 1) & 15
    column = slot_of - 6 * (fine_of >> 7)
    a3 = jnp.where(
        jnp.logical_and(column >= 0, column < 6),
        interp_weight(fine_of & (S - 1), column), 0.0).astype(BF16)
    wide[...] = a3

    loads[3].wait()

    def pack(zz, carry):
        parts = []
        for zl in range(GROUP):
            z = zz * GROUP + zl
            acc = jnp.zeros((8, 128), F32)
            for g in range(8):
                n = zl * 8 + g
                cell = th[z, 8 + 8 * g:16 + 8 * g, :]
                acc = jnp.where((lane >> 1) == n, pltpu.roll(cell, (2 * n + 1) % 128, 1), acc)
            parts.append(acc)
        while len(parts) > 1:
            parts = [parts[n] + parts[n + 1] for n in range(0, len(parts), 2)]
        acc = parts[0]
        levels = range(GROUP)
        low = jnp.concatenate([th[zz * GROUP + zl, 8:9, :] for zl in levels], axis=0)
        high = jnp.concatenate(
            [th[zz * GROUP + zl, 7 + BX:8 + BX, :] for zl in levels], axis=0)
        rows_of = pl.ds(pl.multiple_of(zz * 8, 8), 8)
        xth_out[0, rows_of, :] = high
        xth_out[1, rows_of, :] = low
        yth_out[rows_of, :] = acc
        return carry

    lax.fori_loop(0, LZ // GROUP, pack, 0)
    halos = []
    for n, (out, into, dx, dy) in enumerate([
        (xth_out.at[0], xth_in.at[0], 1, 0),
        (xth_out.at[1], xth_in.at[1], -1, 0),
        (yth_out, yth_in.at[0], 0, 1),
        (yth_out, yth_in.at[1], 0, -1),
    ]):
        halos.append(pltpu.make_async_remote_copy(
            src_ref=out, dst_ref=into, send_sem=th_send.at[n], recv_sem=th_recv.at[n],
            device_id=(gx(dx), gy(dy)), device_id_type=MESH))
    for copy in halos:
        copy.start()

    for copy in winds:
        copy.wait_recv()
    for copy in requests:
        copy.wait_recv()
    odd = (lane & 1) == 1
    ends = jnp.logical_or(lane == 0, lane == 127)
    is_first = i == 0
    is_last = i == G - 1
    south_ok = jnp.where(j > 0, 1.0, 0.0).astype(F32)
    north_ok = jnp.where(j < H - 1, 1.0, 0.0).astype(F32)
    west_ok = jnp.where(i > 0, 1.0, 0.0).astype(F32)
    east_ok = jnp.where(i < G - 1, 1.0, 0.0).astype(F32)

    def both(south, north):
        return jnp.where(odd, north * north_ok, south * south_ok)

    def unpack(mixed, n):
        return pltpu.roll(mixed, (127 - 2 * n) % 128, 1)

    sub = iota((8, 128), 0)
    here = both(yw_in[0], yw_in[1])
    east = both(yw_in[2], yw_in[3]) * east_ok
    west = both(yw_in[4], yw_in[5]) * west_ok
    surface = []
    for c, source in ((0, uu), (1, vv)):
        zeros = jnp.zeros((8, 128), F32)
        left = [source[0]]
        right = [jnp.where(ends, unpack(here, 8 * c + g), 0.0) for g in range(8)]
        east_row = req_in[G - 1, 2 + c:3 + c, :] * east_ok
        west_row = req_in[1, 2 + c:3 + c, :] * west_ok
        left.append(jnp.where(sub == 0, east_row, 0.0))
        left += [zeros] * 6
        left.append(jnp.where(sub == 7, west_row, 0.0))
        right.append(jnp.where(jnp.logical_and(ends, sub == 0), unpack(east, 8 * c), 0.0))
        right += [zeros] * 6
        right.append(jnp.where(jnp.logical_and(ends, sub == 7), unpack(west, 8 * c + 7), 0.0))
        surface.append(jnp.concatenate(
            [jnp.concatenate(left, axis=0), jnp.concatenate(right, axis=0)], axis=1))

    lane_q = iota((16, 128), 1)
    k_q = iota((16, 128), 0)
    pick = ([], [])
    masks = []
    later = []
    for q in range(Q):
        place = req_in[q // CAP, q % CAP:q % CAP + 1, :].astype(jnp.int32)
        x0 = (place >> 5) * TA
        y0 = (place & 31) * TA
        for c in range(2):
            m = k_q - 6 * c
            hit = jnp.logical_and(
                lane_q == ((x0 - 1 + m) & 127), jnp.logical_and(m >= 0, m < 6))
            pick[c].append(jnp.where(hit, 1.0, 0.0))
        low = (lane_q - (y0 - 1)) & 255
        high = (lane_q + 128 - (y0 - 1)) & 255
        masks.append(jnp.concatenate(
            [jnp.where(low < 6, 1.0, 0.0), jnp.where(high < 6, 1.0, 0.0)], axis=1))
        later.append(jnp.broadcast_to((y0 & 4) != 0, (16, 128)))
    found = (dot_left_exact(jnp.concatenate(pick[0], axis=0), surface[0])
             + dot_left_exact(jnp.concatenate(pick[1], axis=0), surface[1]))
    found = found * jnp.concatenate(masks, axis=0)
    c_e = iota((256, 256), 0)
    l_e = iota((256, 256), 1)
    shift = jnp.where(l_e < 128, 1, 5)
    squeeze = jnp.where(((c_e + shift) & 7) == (l_e & 7), 1.0, 0.0)
    tight = dot_right_exact(found, squeeze)
    own_lanes = (lane_q >> 3) == k_q
    for q in range(Q):
        block = tight[16 * q:16 * q + 16]
        chosen = jnp.where(later[q], block[:, 128:], block[:, :128])
        rep_out[q // CAP, q % CAP:q % CAP + 1, :] = jnp.sum(
            jnp.where(own_lanes, chosen, 0.0), axis=0, keepdims=True)
    replies = [
        to_peer(-o, rep_out.at[o], rep_in.at[o], rep_send.at[o], rep_recv.at[o])
        for o in range(1, G)
    ]
    for copy in replies:
        copy.start()
    rep_in[0] = rep_out[0]

    def advect(zz, carry):
        rows_of = pl.ds(pl.multiple_of(zz * 8, 8), 8)
        mixed = both(yth_in[0, rows_of, :], yth_in[1, rows_of, :])
        lane_x = iota((BX, 128), 1)
        for first in range(0, GROUP, 2):
            done = []
            for zl in (first, first + 1):
                z = zz * GROUP + zl
                centre = th[z, 8:8 + BX, :]
                before = th[z, 7:7 + BX, :]
                after = th[z, 9:9 + BX, :]
                edge = jnp.concatenate([unpack(mixed, zl * 8 + g) for g in range(8)], axis=0)
                south = pltpu.roll(jnp.where(lane_x == 127, edge, centre), 1, 1)
                north = pltpu.roll(jnp.where(lane_x == 0, edge, centre), 127, 1)
                u = uu[z]
                v = vv[z]
                total = (jnp.maximum(u, 0.0) * (centre - before)
                         + jnp.minimum(u, 0.0) * (after - centre)
                         + jnp.maximum(v, 0.0) * (centre - south)
                         + jnp.minimum(v, 0.0) * (north - centre))
                done.append((z, centre - 0.4 * total))
            for z, value in done:
                part[z] = value
        store(zz).start()
        return carry

    def store(zz):
        levels = pl.ds(zz * GROUP, GROUP)
        return pltpu.make_async_copy(part.at[levels], part_hbm.at[levels], part_sem.at[zz])

    groups = LZ // GROUP
    first_groups = groups // 2
    for copy in halos:
        copy.wait_recv()
    loads[4].wait()
    loads[5].wait()

    def rim(zz, carry):
        rows_of = pl.ds(pl.multiple_of(zz * 8, 8), 8)
        low = xth_in[0, rows_of, :] * west_ok
        high = xth_in[1, rows_of, :] * east_ok
        for zl in range(GROUP):
            z = zz * GROUP + zl
            th[z, 7:8, :] = low[zl:zl + 1]
            th[z, 8 + BX:9 + BX, :] = high[zl:zl + 1]
        return carry

    lax.fori_loop(0, groups, rim, 0)
    lax.fori_loop(0, first_groups, advect, 0)

    for copy in replies:
        copy.wait_recv()
    answers = jnp.concatenate([rep_in[o] for o in range(G)], axis=0)
    is_slot = jnp.where(code_col[:, :Q] == iota((TPD, Q), 1), 1.0, 0.0)
    patch = dot_left_exact(is_slot, answers)
    spread = jnp.concatenate(
        [jnp.where(own_lanes, patch[t:t + 1], 0.0) for t in range(TPD)], axis=0)
    by_y = jnp.where(
        (iota((128, 128), 0) & 7) < 6,
        interp_weight(iota((128, 128), 1), iota((128, 128), 0) & 7), 0.0)
    along_y = dot_right_exact(spread, by_y)
    high, middle, low = pieces(along_y)
    for t in range(TPD):
        small[t, 0:16, :] = high[16 * t:16 * t + 16]
        small[t, 16:32, :] = middle[16 * t:16 * t + 16]
        small[t, 32:48, :] = low[16 * t:16 * t + 16]

    for load in loads[6:]:
        load.wait()
    pair = 2
    lane_c = iota((R, 128), 1)
    first_lane = lane_c == 0
    last_lane = lane_c == 127

    def level_store(t):
        return pltpu.make_async_copy(lout.at[t], level_out.at[0, 0, t], lev_sem.at[t])

    def fuel_store(t):
        return pltpu.make_async_copy(fout.at[t], fuel_out.at[0, 0, t], fuel_sem.at[t])

    def pad_tile(t, carry):
        lev[t, 7:8, :] = lev[t, 8:9, :]
        lev[t, 8 + S:9 + S, :] = lev[t, 7 + S:8 + S, :]
        return carry

    lax.fori_loop(0, TPD, pad_tile, 0)

    def fire(step, carry):
        for p in range(pair):
            t = step * pair + p
            wind[p] = dot(wide[...], small[t])
            for b in range(S // R):
                strength = 0.015 * base[t, R * b:R * b + R, :]
                scaled[p, R * b:R * b + R, :] = strength
                wind[p, R * b:R * b + R, :] = wind[p, R * b:R * b + R, :] * strength
                wind[p, S + R * b:S + R * b + R, :] = (
                    wind[p, S + R * b:S + R * b + R, :] * strength)
        for k in range(KSUB):
            last = k == KSUB - 1
            for p in range(pair):
                t = step * pair + p
                old = lev.at[t] if k == 0 else (ping, pong)[(k - 1) % 2].at[p]
                new = (ping, pong)[k % 2].at[p]
                fuel_old = fin.at[t] if k == 0 else burn.at[p]
                for b in range(S // R):
                    at = 8 + R * b
                    here_b = slice(R * b, R * b + R)
                    centre = old[at:at + R, :]
                    before = old[at - 1:at - 1 + R, :]
                    after = old[at + 1:at + 1 + R, :]
                    left = jnp.where(first_lane, centre, pltpu.roll(centre, 1, 1))
                    right = jnp.where(last_lane, centre, pltpu.roll(centre, 127, 1))
                    dx = after - before
                    dy = right - left
                    around = (after + before) + (right + left)
                    square = (dx * dx + 0.04) + dy * dy
                    length = square * lax.rsqrt(square)
                    blown = (wind[p, R * b:R * b + R, :] * dx
                             + wind[p, S + R * b:S + R * b + R, :] * dy)
                    rate = jnp.maximum(scaled[p, here_b, :] * length + blown, 0.0)
                    level = (0.4 * centre + 0.15 * around) - rate
                    fuel = fuel_old[here_b, :] * (0.925 + 0.075 * jnp.tanh(level))
                    if last:
                        lout[t, here_b, :] = level
                        fout[t, here_b, :] = fuel
                        burnt = fin[t, here_b, :] - fuel
                        rows[b, pl.ds(t, 1), :] = jnp.sum(burnt, axis=0, keepdims=True)
                    else:
                        new[at:at + R, :] = level
                        if b == 0:
                            new[7:8, :] = level[0:1]
                        if b == S // R - 1:
                            new[8 + S:9 + S, :] = level[R - 1:R]
                        burn[p, here_b, :] = fuel
        for p in range(pair):
            t = step * pair + p
            level_store(t).start()
            fuel_store(t).start()
        return carry

    lax.fori_loop(0, TPD // pair, fire, 0)

    l_m = iota((128, 128), 0)
    c_m = iota((128, 128), 1)
    mean = jnp.where((l_m >> 5) == (c_m & 3), 1.0 / (R * R), 0.0)
    fluxes = dot_right_exact(jnp.concatenate([rows[b] for b in range(TA)], axis=0), mean)
    slot_rows = iota((Q * TA, 64), 0)
    slot_lanes = iota((Q * TA, 64), 1)
    to_slot = jnp.where(
        jnp.logical_and(code_row[0:1, :64] == (slot_rows >> 2),
                        (slot_lanes >> 4) == (slot_rows & 3)), 1.0, 0.0)
    sent = dot_left_exact(to_slot, fluxes)
    for o in range(G):
        flux_out[o] = sent[8 * o:8 * o + 8]
    returned = [
        to_peer(o, flux_out.at[o], flux_in.at[o], flux_send.at[o], flux_recv.at[o])
        for o in range(1, G)
    ]
    for copy in returned:
        copy.start()
    flux_in[0] = flux_out[0]

    lax.fori_loop(first_groups, groups, advect, 0)

    lane8 = lane
    row8 = sub
    where_x = []
    where_y = []
    for o in range(G):
        p0 = req_in[o, 0:1, :].astype(jnp.int32)
        p1 = req_in[o, 1:2, :].astype(jnp.int32)
        place = jnp.where(row8 < TA, p0, p1)
        x0 = (place >> 5) * TA
        where_x.append(jnp.where(lane8 == x0 + (row8 & 3), 1.0, 0.0))
        where_y.append((lane8 >> 2) == (place & 31))
    across = jnp.concatenate(where_x, axis=0).T
    for copy in returned:
        copy.wait_recv()
    values = jnp.concatenate(
        [jnp.where(where_y[o], flux_in[o], 0.0) for o in range(G)], axis=0)
    field_ref[...] = dot_left_exact(across, values)[:BX]

    for copy in requests + winds + halos + replies + returned:
        copy.wait_send()

    def finish_tile(t, carry):
        level_store(t).wait()
        fuel_store(t).wait()
        return carry

    lax.fori_loop(0, TPD, finish_tile, 0)

    def finish_group(zz, carry):
        store(zz).wait()
        return carry

    lax.fori_loop(0, groups, finish_group, 0)


def body(G, H, theta, wind_u, wind_v, level_set, fuel_load, spread_base, tile_owner, tile_place):
    LZ = theta.shape[0]
    assert theta.shape[1:] == (BX, BY) and level_set.shape[2:] == (TPD, S, S)
    anywhere = pl.BlockSpec(memory_space=pl.ANY)
    far = pl.BlockSpec(memory_space=pltpu.HBM)
    vmem = pl.BlockSpec(memory_space=pltpu.VMEM)
    dma = pltpu.SemaphoreType.DMA
    scratch = [
        pltpu.VMEM((LZ, BX + 16, BY), F32),
        pltpu.VMEM((LZ, BX, BY), F32),
        pltpu.VMEM((LZ, BX, BY), F32),
        pltpu.VMEM((LZ, BX, BY), F32),
        pltpu.VMEM((TPD, S + 16, S), F32),
        pltpu.VMEM((TPD, S, S), F32),
        pltpu.VMEM((2, S + 16, S), F32),
        pltpu.VMEM((2, S + 16, S), F32),
        pltpu.VMEM((TPD, S, S), F32),
        pltpu.VMEM((2, S, S), F32),
        pltpu.VMEM((TPD, S, S), F32),
        pltpu.VMEM((TPD, S, S), F32),
        pltpu.VMEM((2, 2 * S, S), F32),
        pltpu.VMEM((2, S, S), F32),
        pltpu.VMEM((2 * S, 48), BF16),
        pltpu.VMEM((TPD, 48, S), BF16),
        pltpu.VMEM((TA, TPD, S), F32),
        pltpu.VMEM((TPD, 128), jnp.int32),
        pltpu.SMEM((1, 2, TPD), jnp.int32),
        pltpu.VMEM((G, 4, 128), F32),
        pltpu.VMEM((G, 4, 128), F32),
        pltpu.VMEM((G, 2, 128), F32),
        pltpu.VMEM((G, 2, 128), F32),
        pltpu.VMEM((G, 8, 128), F32),
        pltpu.VMEM((G, 8, 128), F32),
        pltpu.VMEM((8, 128), F32),
        pltpu.VMEM((6, 8, 128), F32),
        pltpu.VMEM((LZ, 128), F32),
        pltpu.VMEM((2, LZ, 128), F32),
        pltpu.VMEM((2, LZ, 128), F32),
        pltpu.VMEM((2, LZ, 128), F32),
        dma((9,)), dma((TPD,)), dma((TPD,)), dma((LZ // GROUP,)),
        dma((G,)), dma((G,)), dma((G,)), dma((G,)), dma((G,)), dma((G,)),
        dma((6,)), dma((6,)), dma((4,)), dma((4,)),
    ]
    part, level_next, fuel_next, field = pl.pallas_call(
        functools.partial(kernel, G, H, LZ),
        out_shape=(
            jax.ShapeDtypeStruct(theta.shape, F32),
            jax.ShapeDtypeStruct(level_set.shape, F32),
            jax.ShapeDtypeStruct(level_set.shape, F32),
            jax.ShapeDtypeStruct((BX, BY), F32),
        ),
        in_specs=[far] * 7,
        out_specs=(anywhere, anywhere, anywhere, vmem),
        scratch_shapes=scratch,
        compiler_params=pltpu.CompilerParams(
            collective_id=0, has_side_effects=True, vmem_limit_bytes=51 * 1024 * 1024),
    )(theta, wind_u, wind_v, level_set, fuel_load, spread_base,
      jnp.concatenate([tile_owner, tile_place], axis=1))
    profile = 2.0 * jnp.exp(-(jnp.arange(LZ, dtype=F32) + 0.5) / (LZ / 4.0))
    theta_next = part + field[None, :, :] * profile[:, None, None]
    return (theta_next, level_next, fuel_next)


def solution(mesh):
    columns = P(None, "gx", "gy")
    tiles = P("gx", "gy", None, None, None)
    lists = P("gx", "gy", None)
    return jax.shard_map(
        functools.partial(body, mesh.shape["gx"], mesh.shape["gy"]),
        mesh=mesh,
        in_specs=(columns, columns, columns, tiles, tiles, tiles, lists, lists),
        out_specs=(columns, tiles, tiles),
        check_vma=False,
    )
```

```python
import functools

import jax
import jax.numpy as jnp
from jax import lax
from jax.experimental import pallas as pl
from jax.experimental.pallas import tpu as pltpu
from jax.sharding import PartitionSpec as P

TA = 4
R = 32
KSUB = 6
CAP = 2
TPD = 16
S = 128
BX = 64
BY = 128
GROUP = 8

MESH = pl.DeviceIdType.MESH
F32 = jnp.float32
BF16 = jnp.bfloat16


def iota(shape, dim):
    return lax.broadcasted_iota(jnp.int32, shape, dim)


def pieces(x):
    high = x.astype(BF16)
    return (high, (x - high.astype(F32)).astype(BF16))


def dot(a, b):
    return jnp.dot(a, b, preferred_element_type=F32)


def dot_left_exact(a, b):
    a = a.astype(BF16)
    high, low = pieces(b)
    return dot(a, high) + dot(a, low)


def dot_right_exact(a, b):
    b = b.astype(BF16)
    high, low = pieces(a)
    return dot(high, b) + dot(low, b)


def interp_weight(fine, column):
    where_fine = (fine.astype(F32) + 0.5) / R + 0.5
    return jnp.maximum(0.0, 1.0 - jnp.abs(where_fine - column.astype(F32)))


def kernel(
    G, H, LZ,
    theta_hbm, u_hbm, v_hbm, level_hbm, fuel_hbm, base_hbm, lists_hbm,
    part_hbm, level_out, fuel_out, field_ref,
    th, uu, vv, part, lev, lout, ping, pong, fin, burn, fout, base, wind, scaled,
    wide, small, rows, code_col, lists,
    req_out, req_in, rep_out, rep_in, flux_out, flux_in,
    yw_out, yw_in, yth_out, yth_in, xth_out, xth_in,
    in_sem, lev_sem, fuel_sem, part_sem,
    req_send, req_recv, rep_send, rep_recv, flux_send, flux_recv,
    yw_send, yw_recv, th_send, th_recv,
):
    Q = G * CAP
    i = lax.axis_index("gx")
    j = lax.axis_index("gy")

    def gx(offset):
        return lax.rem(i + (offset % G), G)

    def gy(offset):
        return lax.rem(j + (offset % H), H)

    loads = [
        pltpu.make_async_copy(lists_hbm, lists, in_sem.at[8]),
        pltpu.make_async_copy(u_hbm.at[0], uu.at[0], in_sem.at[0]),
        pltpu.make_async_copy(v_hbm.at[0], vv.at[0], in_sem.at[1]),
        pltpu.make_async_copy(theta_hbm, th.at[:, 8:8 + BX, :], in_sem.at[2]),
        pltpu.make_async_copy(u_hbm.at[1:], uu.at[1:], in_sem.at[3]),
        pltpu.make_async_copy(v_hbm.at[1:], vv.at[1:], in_sem.at[4]),
        pltpu.make_async_copy(level_hbm.at[0, 0], lev.at[:, 8:8 + S, :], in_sem.at[5]),
        pltpu.make_async_copy(fuel_hbm.at[0, 0], fin, in_sem.at[6]),
        pltpu.make_async_copy(base_hbm.at[0, 0], base, in_sem.at[7]),
    ]
    for load in loads[:4]:
        load.start()

    corners = [(0, 1), (0, -1), (-1, 1), (-1, -1), (1, 1), (1, -1)]
    barrier = pltpu.get_barrier_semaphore()
    for o in range(1, G):
        pl.semaphore_signal(barrier, inc=1, device_id=(gx(o), j), device_id_type=MESH)
    for dx, dy in corners:
        pl.semaphore_signal(barrier, inc=1, device_id=(gx(dx), gy(dy)), device_id_type=MESH)

    loads[0].wait()
    lane = iota((8, 128), 1)
    lane16 = lane & (TPD - 1)
    sub16 = iota((TPD, 128), 0)
    own_row = jnp.zeros((8, 128), jnp.int32)
    place_row = jnp.zeros((8, 128), jnp.int32)
    own_col = jnp.zeros((TPD, 128), jnp.int32)
    for t in range(TPD):
        own_row = jnp.where(lane16 == t, lists[0, 0, t], own_row)
        place_row = jnp.where(lane16 == t, lists[0, 1, t], place_row)
        own_col = jnp.where(sub16 == t, lists[0, 0, t], own_col)
    rank_row = jnp.zeros((8, 128), jnp.int32)
    rank_col = jnp.zeros((TPD, 128), jnp.int32)
    for t in range(TPD):
        rank_row += jnp.where(
            jnp.logical_and(own_row == lists[0, 0, t], lane16 > t), 1, 0)
        rank_col += jnp.where(
            jnp.logical_and(own_col == lists[0, 0, t], sub16 > t), 1, 0)

    def code_of(owner, rank):
        away = owner - i
        return jnp.where(away < 0, away + G, away) * CAP + rank

    code_row = code_of(own_row, rank_row)
    code_col[...] = code_of(own_col, rank_col)

    row1 = code_row[0:1]
    place1 = place_row[0:1]
    wanted = jnp.where(
        jnp.logical_and(row1 == iota((Q, 128), 0), iota((Q, 128), 1) < TPD),
        place1 + 1, 0).astype(F32)
    asked = jnp.broadcast_to(jnp.sum(wanted, axis=1, keepdims=True) - 1.0, (Q, 128))

    loads[1].wait()
    loads[2].wait()
    for o in range(G):
        req_out[o, 0:2, :] = asked[2 * o:2 * o + 2]
        edge = 0 if o == G - 1 else BX - 1
        req_out[o, 2:3, :] = uu[0, edge:edge + 1, :]
        req_out[o, 3:4, :] = vv[0, edge:edge + 1, :]
    packed = jnp.zeros((8, 128), F32)
    for g in range(16):
        source = uu if g < 8 else vv
        cell = source[0, 8 * (g % 8):8 * (g % 8) + 8, :]
        packed = jnp.where((lane >> 1) == g, pltpu.roll(cell, 2 * g + 1, 1), packed)
    yw_out[...] = packed

    pl.semaphore_wait(barrier, G - 1 + len(corners))

    def to_peer(o, out, into, send, recv):
        return pltpu.make_async_remote_copy(
            src_ref=out, dst_ref=into, send_sem=send, recv_sem=recv,
            device_id=(gx(o), j), device_id_type=MESH)

    requests = [
        to_peer(o, req_out.at[o], req_in.at[o], req_send.at[o], req_recv.at[o])
        for o in range(1, G)
    ]
    winds = [
        pltpu.make_async_remote_copy(
            src_ref=yw_out, dst_ref=yw_in.at[n], send_sem=yw_send.at[n],
            recv_sem=yw_recv.at[n], device_id=(gx(dx), gy(dy)), device_id_type=MESH)
        for n, (dx, dy) in enumerate(corners)
    ]
    for copy in requests + winds:
        copy.start()
    req_in[0] = req_out[0]

    fine_of = iota((2 * S, 32), 0)
    slot_of = iota((2 * S, 32), 1) & 15
    column = slot_of - 6 * (fine_of >> 7)
    a3 = jnp.where(
        jnp.logical_and(column >= 0, column < 6),
        interp_weight(fine_of & (S - 1), column), 0.0).astype(BF16)
    wide[...] = a3

    loads[3].wait()
    for load in loads[4:6]:
        load.start()

    def pack(zz, carry):
        parts = []
        for zl in range(GROUP):
            z = zz * GROUP + zl
            acc = jnp.zeros((8, 128), F32)
            for g in range(8):
                n = zl * 8 + g
                cell = th[z, 8 + 8 * g:16 + 8 * g, :]
                acc = jnp.where((lane >> 1) == n, pltpu.roll(cell, (2 * n + 1) % 128, 1), acc)
            parts.append(acc)
        while len(parts) > 1:
            parts = [parts[n] + parts[n + 1] for n in range(0, len(parts), 2)]
        acc = parts[0]
        levels = range(GROUP)
        low = jnp.concatenate([th[zz * GROUP + zl, 8:9, :] for zl in levels], axis=0)
        high = jnp.concatenate(
            [th[zz * GROUP + zl, 7 + BX:8 + BX, :] for zl in levels], axis=0)
        rows_of = pl.ds(pl.multiple_of(zz * 8, 8), 8)
        xth_out[0, rows_of, :] = high
        xth_out[1, rows_of, :] = low
        yth_out[rows_of, :] = acc
        return carry

    lax.fori_loop(0, LZ // GROUP, pack, 0)
    for load in loads[6:]:
        load.start()
    halos = []
    for n, (out, into, dx, dy) in enumerate([
        (xth_out.at[0], xth_in.at[0], 1, 0),
        (xth_out.at[1], xth_in.at[1], -1, 0),
        (yth_out, yth_in.at[0], 0, 1),
        (yth_out, yth_in.at[1], 0, -1),
    ]):
        halos.append(pltpu.make_async_remote_copy(
            src_ref=out, dst_ref=into, send_sem=th_send.at[n], recv_sem=th_recv.at[n],
            device_id=(gx(dx), gy(dy)), device_id_type=MESH))
    for copy in halos:
        copy.start()

    for copy in winds:
        copy.wait_recv()
    for copy in requests:
        copy.wait_recv()
    odd = (lane & 1) == 1
    ends = jnp.logical_or(lane == 0, lane == 127)
    is_first = i == 0
    is_last = i == G - 1
    south_ok = jnp.where(j > 0, 1.0, 0.0).astype(F32)
    north_ok = jnp.where(j < H - 1, 1.0, 0.0).astype(F32)
    west_ok = jnp.where(i > 0, 1.0, 0.0).astype(F32)
    east_ok = jnp.where(i < G - 1, 1.0, 0.0).astype(F32)

    def both(south, north):
        return jnp.where(odd, north * north_ok, south * south_ok)

    def unpack(mixed, n):
        return pltpu.roll(mixed, (127 - 2 * n) % 128, 1)

    sub = iota((8, 128), 0)
    here = both(yw_in[0], yw_in[1])
    east = both(yw_in[2], yw_in[3]) * east_ok
    west = both(yw_in[4], yw_in[5]) * west_ok
    surface = []
    for c, source in ((0, uu), (1, vv)):
        zeros = jnp.zeros((8, 128), F32)
        left = [source[0]]
        right = [jnp.where(ends, unpack(here, 8 * c + g), 0.0) for g in range(8)]
        east_row = req_in[G - 1, 2 + c:3 + c, :] * east_ok
        west_row = req_in[1, 2 + c:3 + c, :] * west_ok
        left.append(jnp.where(sub == 0, east_row, 0.0))
        left += [zeros] * 6
        left.append(jnp.where(sub == 7, west_row, 0.0))
        right.append(jnp.where(jnp.logical_and(ends, sub == 0), unpack(east, 8 * c), 0.0))
        right += [zeros] * 6
        right.append(jnp.where(jnp.logical_and(ends, sub == 7), unpack(west, 8 * c + 7), 0.0))
        surface.append(jnp.concatenate(
            [jnp.concatenate(left, axis=0), jnp.concatenate(right, axis=0)], axis=1))

    lane_q = iota((16, 128), 1)
    k_q = iota((16, 128), 0)
    pick = ([], [])
    masks = []
    later = []
    for q in range(Q):
        place = req_in[q // CAP, q % CAP:q % CAP + 1, :].astype(jnp.int32)
        x0 = (place >> 5) * TA
        y0 = (place & 31) * TA
        for c in range(2):
            m = k_q - 6 * c
            hit = jnp.logical_and(
                lane_q == ((x0 - 1 + m) & 127), jnp.logical_and(m >= 0, m < 6))
            pick[c].append(jnp.where(hit, 1.0, 0.0))
        low = (lane_q - (y0 - 1)) & 255
        high = (lane_q + 128 - (y0 - 1)) & 255
        masks.append(jnp.concatenate(
            [jnp.where(low < 6, 1.0, 0.0), jnp.where(high < 6, 1.0, 0.0)], axis=1))
        later.append(jnp.broadcast_to((y0 & 4) != 0, (16, 128)))
    found = (dot_left_exact(jnp.concatenate(pick[0], axis=0), surface[0])
             + dot_left_exact(jnp.concatenate(pick[1], axis=0), surface[1]))
    found = found * jnp.concatenate(masks, axis=0)
    c_e = iota((256, 256), 0)
    l_e = iota((256, 256), 1)
    shift = jnp.where(l_e < 128, 1, 5)
    squeeze = jnp.where(((c_e + shift) & 7) == (l_e & 7), 1.0, 0.0)
    tight = dot_right_exact(found, squeeze)
    own_lanes = (lane_q >> 3) == k_q
    for q in range(Q):
        block = tight[16 * q:16 * q + 16]
        chosen = jnp.where(later[q], block[:, 128:], block[:, :128])
        rep_out[q // CAP, q % CAP:q % CAP + 1, :] = jnp.sum(
            jnp.where(own_lanes, chosen, 0.0), axis=0, keepdims=True)
    replies = [
        to_peer(-o, rep_out.at[o], rep_in.at[o], rep_send.at[o], rep_recv.at[o])
        for o in range(1, G)
    ]
    for copy in replies:
        copy.start()
    rep_in[0] = rep_out[0]

    def advect(zz, carry):
        rows_of = pl.ds(pl.multiple_of(zz * 8, 8), 8)
        mixed = both(yth_in[0, rows_of, :], yth_in[1, rows_of, :])
        lane_x = iota((BX, 128), 1)
        for first in range(0, GROUP, 4):
            done = []
            for zl in range(first, first + 4):
                z = zz * GROUP + zl
                centre = th[z, 8:8 + BX, :]
                before = th[z, 7:7 + BX, :]
                after = th[z, 9:9 + BX, :]
                edge = jnp.concatenate([unpack(mixed, zl * 8 + g) for g in range(8)], axis=0)
                south = pltpu.roll(jnp.where(lane_x == 127, edge, centre), 1, 1)
                north = pltpu.roll(jnp.where(lane_x == 0, edge, centre), 127, 1)
                u = uu[z]
                v = vv[z]
                total = (jnp.maximum(u, 0.0) * (centre - before)
                         + jnp.minimum(u, 0.0) * (after - centre)
                         + jnp.maximum(v, 0.0) * (centre - south)
                         + jnp.minimum(v, 0.0) * (north - centre))
                done.append((z, centre - 0.4 * total))
            for z, value in done:
                part[z] = value
        store(zz).start()
        return carry

    def store(zz):
        levels = pl.ds(zz * GROUP, GROUP)
        return pltpu.make_async_copy(part.at[levels], part_hbm.at[levels], part_sem.at[zz])

    groups = LZ // GROUP
    first_groups = groups // 2
    for copy in halos:
        copy.wait_recv()
    loads[4].wait()
    loads[5].wait()

    def rim(zz, carry):
        rows_of = pl.ds(pl.multiple_of(zz * 8, 8), 8)
        low = xth_in[0, rows_of, :] * west_ok
        high = xth_in[1, rows_of, :] * east_ok
        for zl in range(GROUP):
            z = zz * GROUP + zl
            th[z, 7:8, :] = low[zl:zl + 1]
            th[z, 8 + BX:9 + BX, :] = high[zl:zl + 1]
        return carry

    lax.fori_loop(0, groups, rim, 0)
    lax.fori_loop(0, first_groups, advect, 0)

    for copy in replies:
        copy.wait_recv()
    answers = jnp.concatenate([rep_in[o] for o in range(G)], axis=0)
    is_slot = jnp.where(code_col[:, :Q] == iota((TPD, Q), 1), 1.0, 0.0)
    patch = dot_left_exact(is_slot, answers)
    spread = jnp.concatenate(
        [jnp.where(own_lanes, patch[t:t + 1], 0.0) for t in range(TPD)], axis=0)
    by_y = jnp.where(
        (iota((128, 128), 0) & 7) < 6,
        interp_weight(iota((128, 128), 1), iota((128, 128), 0) & 7), 0.0)
    along_y = dot_right_exact(spread, by_y)
    high, low = pieces(along_y)
    for t in range(TPD):
        small[t, 0:16, :] = high[16 * t:16 * t + 16]
        small[t, 16:32, :] = low[16 * t:16 * t + 16]

    for load in loads[6:]:
        load.wait()
    pair = 2
    lane_c = iota((R, 128), 1)
    first_lane = lane_c == 0
    last_lane = lane_c == 127

    def level_store(t):
        return pltpu.make_async_copy(lout.at[t], level_out.at[0, 0, t], lev_sem.at[t])

    def fuel_store(t):
        return pltpu.make_async_copy(fout.at[t], fuel_out.at[0, 0, t], fuel_sem.at[t])

    def pad_tile(t, carry):
        lev[t, 7:8, :] = lev[t, 8:9, :]
        lev[t, 8 + S:9 + S, :] = lev[t, 7 + S:8 + S, :]
        return carry

    lax.fori_loop(0, TPD, pad_tile, 0)

    def fire(step, carry):
        for p in range(pair):
            t = step * pair + p
            wind[p] = dot(wide[...], small[t])
            for b in range(S // R):
                strength = 0.015 * base[t, R * b:R * b + R, :]
                scaled[p, R * b:R * b + R, :] = strength
                wind[p, R * b:R * b + R, :] = wind[p, R * b:R * b + R, :] * strength
                wind[p, S + R * b:S + R * b + R, :] = (
                    wind[p, S + R * b:S + R * b + R, :] * strength)
        for k in range(KSUB):
            last = k == KSUB - 1
            for p in range(pair):
                t = step * pair + p
                old = lev.at[t] if k == 0 else (ping, pong)[(k - 1) % 2].at[p]
                new = (ping, pong)[k % 2].at[p]
                fuel_old = fin.at[t] if k == 0 else burn.at[p]
                for b in range(S // R):
                    at = 8 + R * b
                    here_b = slice(R * b, R * b + R)
                    centre = old[at:at + R, :]
                    before = old[at - 1:at - 1 + R, :]
                    after = old[at + 1:at + 1 + R, :]
                    left = jnp.where(first_lane, centre, pltpu.roll(centre, 1, 1))
                    right = jnp.where(last_lane, centre, pltpu.roll(centre, 127, 1))
                    dx = after - before
                    dy = right - left
                    around = (after + before) + (right + left)
                    square = (dx * dx + 0.04) + dy * dy
                    length = square * lax.rsqrt(square)
                    blown = (wind[p, R * b:R * b + R, :] * dx
                             + wind[p, S + R * b:S + R * b + R, :] * dy)
                    rate = jnp.maximum(scaled[p, here_b, :] * length + blown, 0.0)
                    level = (0.4 * centre + 0.15 * around) - rate
                    fuel = fuel_old[here_b, :] * (0.925 + 0.075 * jnp.tanh(level))
                    if last:
                        lout[t, here_b, :] = level
                        fout[t, here_b, :] = fuel
                        burnt = fin[t, here_b, :] - fuel
                        rows[b, pl.ds(t, 1), :] = jnp.sum(burnt, axis=0, keepdims=True)
                    else:
                        new[at:at + R, :] = level
                        if b == 0:
                            new[7:8, :] = level[0:1]
                        if b == S // R - 1:
                            new[8 + S:9 + S, :] = level[R - 1:R]
                        burn[p, here_b, :] = fuel
        for p in range(pair):
            t = step * pair + p
            level_store(t).start()
            fuel_store(t).start()
        return carry

    lax.fori_loop(0, TPD // pair, fire, 0)

    l_m = iota((128, 128), 0)
    c_m = iota((128, 128), 1)
    mean = jnp.where((l_m >> 5) == (c_m & 3), 1.0 / (R * R), 0.0)
    fluxes = dot_right_exact(jnp.concatenate([rows[b] for b in range(TA)], axis=0), mean)
    slot_rows = iota((Q * TA, 64), 0)
    slot_lanes = iota((Q * TA, 64), 1)
    to_slot = jnp.where(
        jnp.logical_and(code_row[0:1, :64] == (slot_rows >> 2),
                        (slot_lanes >> 4) == (slot_rows & 3)), 1.0, 0.0)
    sent = dot_left_exact(to_slot, fluxes)
    for o in range(G):
        flux_out[o] = sent[8 * o:8 * o + 8]
    returned = [
        to_peer(o, flux_out.at[o], flux_in.at[o], flux_send.at[o], flux_recv.at[o])
        for o in range(1, G)
    ]
    for copy in returned:
        copy.start()
    flux_in[0] = flux_out[0]

    lax.fori_loop(first_groups, groups, advect, 0)

    lane8 = lane
    row8 = sub
    where_x = []
    where_y = []
    for o in range(G):
        p0 = req_in[o, 0:1, :].astype(jnp.int32)
        p1 = req_in[o, 1:2, :].astype(jnp.int32)
        place = jnp.where(row8 < TA, p0, p1)
        x0 = (place >> 5) * TA
        where_x.append(jnp.where(lane8 == x0 + (row8 & 3), 1.0, 0.0))
        where_y.append((lane8 >> 2) == (place & 31))
    across = jnp.concatenate(where_x, axis=0).T
    for copy in returned:
        copy.wait_recv()
    values = jnp.concatenate(
        [jnp.where(where_y[o], flux_in[o], 0.0) for o in range(G)], axis=0)
    field_ref[...] = dot_left_exact(across, values)[:BX]

    for copy in requests + winds + halos + replies + returned:
        copy.wait_send()

    def finish_tile(t, carry):
        level_store(t).wait()
        fuel_store(t).wait()
        return carry

    lax.fori_loop(0, TPD, finish_tile, 0)

    def finish_group(zz, carry):
        store(zz).wait()
        return carry

    lax.fori_loop(0, groups, finish_group, 0)


def body(G, H, theta, wind_u, wind_v, level_set, fuel_load, spread_base, tile_owner, tile_place):
    LZ = theta.shape[0]
    assert theta.shape[1:] == (BX, BY) and level_set.shape[2:] == (TPD, S, S)
    anywhere = pl.BlockSpec(memory_space=pl.ANY)
    far = pl.BlockSpec(memory_space=pltpu.HBM)
    vmem = pl.BlockSpec(memory_space=pltpu.VMEM)
    dma = pltpu.SemaphoreType.DMA
    scratch = [
        pltpu.VMEM((LZ, BX + 16, BY), F32),
        pltpu.VMEM((LZ, BX, BY), F32),
        pltpu.VMEM((LZ, BX, BY), F32),
        pltpu.VMEM((LZ, BX, BY), F32),
        pltpu.VMEM((TPD, S + 16, S), F32),
        pltpu.VMEM((TPD, S, S), F32),
        pltpu.VMEM((2, S + 16, S), F32),
        pltpu.VMEM((2, S + 16, S), F32),
        pltpu.VMEM((TPD, S, S), F32),
        pltpu.VMEM((2, S, S), F32),
        pltpu.VMEM((TPD, S, S), F32),
        pltpu.VMEM((TPD, S, S), F32),
        pltpu.VMEM((2, 2 * S, S), F32),
        pltpu.VMEM((2, S, S), F32),
        pltpu.VMEM((2 * S, 32), BF16),
        pltpu.VMEM((TPD, 32, S), BF16),
        pltpu.VMEM((TA, TPD, S), F32),
        pltpu.VMEM((TPD, 128), jnp.int32),
        pltpu.SMEM((1, 2, TPD), jnp.int32),
        pltpu.VMEM((G, 4, 128), F32),
        pltpu.VMEM((G, 4, 128), F32),
        pltpu.VMEM((G, 2, 128), F32),
        pltpu.VMEM((G, 2, 128), F32),
        pltpu.VMEM((G, 8, 128), F32),
        pltpu.VMEM((G, 8, 128), F32),
        pltpu.VMEM((8, 128), F32),
        pltpu.VMEM((6, 8, 128), F32),
        pltpu.VMEM((LZ, 128), F32),
        pltpu.VMEM((2, LZ, 128), F32),
        pltpu.VMEM((2, LZ, 128), F32),
        pltpu.VMEM((2, LZ, 128), F32),
        dma((9,)), dma((TPD,)), dma((TPD,)), dma((LZ // GROUP,)),
        dma((G,)), dma((G,)), dma((G,)), dma((G,)), dma((G,)), dma((G,)),
        dma((6,)), dma((6,)), dma((4,)), dma((4,)),
    ]
    part, level_next, fuel_next, field = pl.pallas_call(
        functools.partial(kernel, G, H, LZ),
        out_shape=(
            jax.ShapeDtypeStruct(theta.shape, F32),
            jax.ShapeDtypeStruct(level_set.shape, F32),
            jax.ShapeDtypeStruct(level_set.shape, F32),
            jax.ShapeDtypeStruct((BX, BY), F32),
        ),
        in_specs=[far] * 7,
        out_specs=(anywhere, anywhere, anywhere, vmem),
        scratch_shapes=scratch,
        compiler_params=pltpu.CompilerParams(
            collective_id=0, has_side_effects=True, vmem_limit_bytes=51 * 1024 * 1024),
    )(theta, wind_u, wind_v, level_set, fuel_load, spread_base,
      jnp.concatenate([tile_owner, tile_place], axis=1))
    profile = 2.0 * jnp.exp(-(jnp.arange(LZ, dtype=F32) + 0.5) / (LZ / 4.0))
    theta_next = part + field[None, :, :] * profile[:, None, None]
    return (theta_next, level_next, fuel_next)


def solution(mesh):
    columns = P(None, "gx", "gy")
    tiles = P("gx", "gy", None, None, None)
    lists = P("gx", "gy", None)
    return jax.shard_map(
        functools.partial(body, mesh.shape["gx"], mesh.shape["gy"]),
        mesh=mesh,
        in_specs=(columns, columns, columns, tiles, tiles, tiles, lists, lists),
        out_specs=(columns, tiles, tiles),
        check_vma=False,
    )
```
